256 devices in a mesh: row: 8 (over z_lo, core), col: 32 (over z_hi, y, x).
Axes of the slice: x: 4, y: 4, z: 8 (z_hi: 2, z_lo: 4; z = z_hi * 4 + z_lo), core: 2. Of those that a mesh axis runs over, the one named last changes fastest.
Arguments:
- tokens: bfloat16 [1024, 16384], P('row', 'col'), may hold values from -6 to 6
- w_query: bfloat16 [16384, 8192], P('col', 'row'), may hold values from -0.078125 to 0.078125
- w_keyval: bfloat16 [16384, 1024], P('col', 'row'), may hold values from -0.078125 to 0.078125
- w_output: bfloat16 [8192, 16384], P('row', 'col'), may hold values from -0.0625 to 0.0625
Outputs:
- result: bfloat16 [1024, 16384], P('row', 'col')
The draws below stay inside these ranges and needn't reach their ends.
All inputs are finite; a program needn't handle non-finite values.
Results may differ from the reference program's by a relative error of at most 0.02.
Values may be sent and summed in bfloat16 or wider, within the bound.
No kernel may reach another device: no remote copies, remote signals or barrier semaphores. Data moves between devices by JAX's collectives and lax.ppermute only.
A program may use at most 64 MiB of HBM per device.

```python
import math
import jax
import jax.numpy as jnp
from jax import lax

D = 16384
HQ = 64
KVH = 4
HD = 128
TOKENS = 1024


def block_levels(own_key, extent, shards, smallest, top_value):
    gain, own = 1.0, jax.random.fold_in(own_key, 6)
    for dim, parts in shards:
        heights = jnp.exp(jax.random.uniform(jax.random.fold_in(own, dim), (parts,), jnp.float32, smallest / len(shards), top_value / len(shards)))
        gain = gain * jnp.repeat(heights, extent[dim] // parts).reshape([-1 if axis == dim else 1 for axis in range(len(extent))])
    return gain


def centred(rng, dims, spread, bound, cuts=(), held_as=jnp.bfloat16):
    result = spread * jax.random.normal(rng, dims, jnp.float32)
    if cuts:
        result = result * block_levels(rng, dims, cuts, -0.22, 0.18)
    return jnp.clip(result, -bound, bound).astype(held_as)


def setup_inputs(seed: int = 0) -> dict:
    splits = jax.random.split(jax.random.key(seed), 5)
    return {
        "tokens": centred(splits[0], (TOKENS, D), 1.0, 6.0, ((0, 8), (1, 32))),
        "w_query": centred(splits[1], (D, HQ * HD), (D // 3) ** -0.5, 0.078125, ((0, 32), (1, 8))),
        "w_keyval": centred(splits[2], (D, 2 * KVH * HD), (D // 3) ** -0.5, 0.078125, ((0, 32), (1, 8))),
        "w_output": centred(splits[3], (HQ * HD, D), (HQ * HD) ** -0.5, 0.0625, ((0, 8), (1, 32))),
    }


def angles(positions, width):
    half_width = width // 2
    frequency = 500000.0 ** (-(jnp.arange(half_width).astype(jnp.float32) * 2.0 / width))
    angle_v = positions[:, None] * frequency[None, :]
    return (jnp.cos(angle_v), jnp.sin(angle_v))

def rotate(values_in, cosine, sine_v):
    half_width = values_in.shape[-1] // 2
    lower_half = values_in[..., :half_width]
    upper_half = values_in[..., half_width:]
    return jnp.concatenate([lower_half * cosine - upper_half * sine_v, upper_half * cosine + lower_half * sine_v], -1)

def reference(tokens, w_query, w_keyval, w_output):
    query_sum = jnp.dot(tokens, w_query, preferred_element_type=jnp.float32)
    keyval = jnp.dot(tokens, w_keyval, preferred_element_type=jnp.float32).astype(jnp.bfloat16)
    positions = jnp.arange(TOKENS).astype(jnp.float32)
    cosine, sine_v = angles(positions, HD)
    query = rotate(query_sum.reshape(TOKENS, HQ, HD), cosine[:, None, :], sine_v[:, None, :]).astype(jnp.bfloat16)
    key_part = keyval[:, :KVH * HD].reshape(TOKENS, KVH, HD).astype(jnp.float32)
    keys = rotate(key_part, cosine[:, None, :], sine_v[:, None, :]).astype(jnp.bfloat16)
    values = keyval[:, KVH * HD:].reshape(TOKENS, KVH, HD)
    group_size = HQ // KVH
    score_scale = 1.0 / math.sqrt(HD)
    token_index = jnp.arange(TOKENS, dtype=jnp.int32)
    causal = token_index[None, :] <= token_index[:, None]

    def per_head(head_index):
        key_head = (head_index // group_size).astype(jnp.int32)
        query_head = lax.dynamic_index_in_dim(query, head_index, 1, keepdims=False)
        key_rows = lax.dynamic_index_in_dim(keys, key_head, 1, keepdims=False)
        value_rows = lax.dynamic_index_in_dim(values, key_head, 1, keepdims=False)
        scores = jnp.dot(query_head, key_rows.T, preferred_element_type=jnp.float32) * score_scale
        weights_raw = jnp.where(causal, jnp.exp(jnp.where(causal, scores, 0.0)), 0.0)
        totals = lax.optimization_barrier(jnp.sum(weights_raw, -1, keepdims=True))
        weights_b = weights_raw.astype(jnp.bfloat16)
        mixed = jnp.dot(weights_b, value_rows, preferred_element_type=jnp.float32) / totals
        return mixed.astype(jnp.bfloat16)
    heads_all = lax.map(per_head, jnp.arange(HQ, dtype=jnp.int32))
    attended = jnp.transpose(heads_all, (1, 0, 2)).reshape(TOKENS, HQ * HD)
    return jnp.dot(attended, w_output, preferred_element_type=jnp.float32).astype(jnp.bfloat16)
```

```python
import math

import jax
import jax.numpy as jnp
from jax import lax
from jax.sharding import Mesh
from jax.sharding import PartitionSpec as P

HD = 128
Z_LO, CORE, Z_HI, Y, X = 4, 2, 2, 4, 4
ROW = ("zl", "core")
COL = ("zh", "y", "x")
PLANE = ("y", "x")
BF16 = jnp.bfloat16
F32 = jnp.float32


def angles(positions, width):
    half_width = width // 2
    frequency = 500000.0 ** (-(jnp.arange(half_width).astype(F32) * 2.0 / width))
    angle_v = positions[:, None] * frequency[None, :]
    return (jnp.cos(angle_v), jnp.sin(angle_v))


def rotate(values_in, cosine, sine_v):
    half_width = values_in.shape[-1] // 2
    lower_half = values_in[..., :half_width]
    upper_half = values_in[..., half_width:]
    return jnp.concatenate(
        [lower_half * cosine - upper_half * sine_v, upper_half * cosine + lower_half * sine_v], -1
    )


def gather(block, axes, count):
    spread = jnp.broadcast_to(block[None], (count, *block.shape))
    return lax.all_to_all(spread, axes, 0, 0, tiled=True)


def swap(block, axis):
    return lax.ppermute(block, axis, ((0, 1), (1, 0)))


def shards(tokens, w_query, w_keyval, w_output):
    core = lax.axis_index("core")
    chunk = lax.axis_index("y") * X + lax.axis_index("x")
    per_row, features = tokens.shape
    half = per_row * Z_LO
    total = half * 2
    per_chunk = total // (Y * X)
    width = w_query.shape[1]
    heads = width // HD

    kv_moves = [(e, 2 * e if e < 4 else 2 * (e - 4) + 1) for e in range(8)]
    w_kv = lax.ppermute(w_keyval, ROW, kv_moves)

    mine = gather(tokens, "zl", Z_LO).reshape(half, features)
    other = swap(mine, "core")
    everyone = jnp.concatenate([mine, other], 0)
    query_part = jnp.dot(everyone, w_query, preferred_element_type=F32).astype(BF16)
    kv_part = jnp.dot(everyone, w_kv, preferred_element_type=F32).astype(BF16)
    part = jnp.concatenate([query_part, kv_part], 1)

    part = part.reshape(Y * X, per_chunk, width + HD)
    part = lax.all_to_all(part, PLANE, 0, 0, tiled=True)
    part = jnp.sum(part.astype(F32), 0).astype(BF16)
    sums = part.astype(F32) + swap(part, "zh").astype(F32)

    def positions(index):
        side = index // half
        inner = index % half
        which = jnp.where(side == 0, core, 1 - core)
        return (inner // per_row) * (2 * per_row) + which * per_row + inner % per_row

    query_pos = positions(chunk * per_chunk + jnp.arange(per_chunk, dtype=jnp.int32))
    key_pos = positions(jnp.arange(total, dtype=jnp.int32))
    cosine, sine_v = angles(query_pos.astype(F32), HD)

    kv_own = sums[:, width:].astype(BF16)
    kv_rot = rotate(kv_own.astype(F32), cosine, sine_v).astype(BF16)
    kv_own = jnp.where(core == 0, kv_rot, kv_own)
    kv_all = gather(kv_own, PLANE, Y * X).reshape(total, HD)
    kv_got = swap(kv_all, "core")
    kv_got = jnp.concatenate([kv_got[half:], kv_got[:half]], 0)
    keys = jnp.where(core == 0, kv_all, kv_got)
    values = jnp.where(core == 0, kv_got, kv_all)

    query = rotate(
        sums[:, :width].reshape(per_chunk, heads, HD), cosine[:, None, :], sine_v[:, None, :]
    ).astype(BF16)
    query = jnp.transpose(query, (1, 0, 2))
    scores = jnp.einsum("htd,sd->hts", query, keys, preferred_element_type=F32) * (
        1.0 / math.sqrt(HD)
    )
    causal = (key_pos[None, :] <= query_pos[:, None])[None]
    weights_raw = jnp.where(causal, jnp.exp(jnp.where(causal, scores, 0.0)), 0.0)
    totals = jnp.sum(weights_raw, -1)
    mixed = jnp.einsum(
        "hts,sd->htd", weights_raw.astype(BF16), values, preferred_element_type=F32
    )
    attended = (mixed / totals[:, :, None]).astype(BF16)
    attended = jnp.transpose(attended, (1, 0, 2)).reshape(per_chunk, width)

    attended_all = gather(attended, PLANE, Y * X).reshape(total, width)
    partial_out = jnp.dot(attended_all, w_output, preferred_element_type=F32).astype(BF16)
    kept, sent = partial_out[:half], partial_out[half:]
    chip = (kept.astype(F32) + swap(sent, "core").astype(F32)).astype(BF16)
    chip = chip.reshape(Z_LO, per_row, features)
    chip = lax.all_to_all(chip, "zl", 0, 0, tiled=True)
    return jnp.sum(chip.astype(F32), 0).astype(BF16)


def solution(mesh):
    fine = Mesh(
        mesh.devices.reshape(Z_LO, CORE, Z_HI, Y, X), ("zl", "core", "zh", "y", "x")
    )
    return jax.shard_map(
        shards,
        mesh=fine,
        in_specs=(P(ROW, COL), P(COL, ROW), P(COL, ROW), P(ROW, COL)),
        out_specs=P(ROW, COL),
        check_vma=False,
    )
```

```python
import functools
import math

import jax
import jax.numpy as jnp
from jax import lax
from jax.experimental import pallas as pl
from jax.experimental.pallas import tpu as pltpu
from jax.sharding import Mesh
from jax.sharding import PartitionSpec as P

HD = 128
Z_LO, CORE, Z_HI, Y, X = 4, 2, 2, 4, 4
ROW = ("zl", "core")
COL = ("zh", "y", "x")
PLANE = ("y", "x")
BF16 = jnp.bfloat16
F32 = jnp.float32
VMEM = pl.BlockSpec(memory_space=pltpu.VMEM)
SMEM = pl.BlockSpec(memory_space=pltpu.SMEM)
PARAMS = pltpu.CompilerParams(vmem_limit_bytes=32 * 1024 * 1024)


def tables(positions, width):
    half_width = width // 2
    frequency = 500000.0 ** (-(jnp.arange(half_width).astype(F32) * 2.0 / width))
    angle_v = positions[:, None] * frequency[None, :]
    cosine, sine_v = jnp.cos(angle_v), jnp.sin(angle_v)
    return jnp.concatenate([cosine, cosine], 1), jnp.concatenate([-sine_v, sine_v], 1)


def rotate(values_in, cosine, sine_v):
    return values_in * cosine + pltpu.roll(values_in, HD // 2, 1) * sine_v


def partner(block, axis, step):
    size = {"zl": Z_LO, "core": CORE, "zh": Z_HI, "y": Y, "x": X}[axis]
    return lax.ppermute(block, axis, [(i, i ^ step) for i in range(size)])


def kv_kernel(pick, *refs):
    blocks, weight, outs, parts = refs[:8], refs[8], refs[9:13], refs[13]
    rows = blocks[0].shape[0]
    for i, block in enumerate(blocks):
        product = jnp.dot(block[...], weight[...], preferred_element_type=F32)
        parts[i // 2, pl.ds((i % 2) * rows, rows), :] = product.astype(BF16)
    for s, out in enumerate(outs):
        out[...] = parts[pick[s]]


def query_kernel(*refs):
    blocks, weight, out = refs[:8], refs[8], refs[9]
    per_chunk = out.shape[1]
    for i, block in enumerate(blocks):
        product = jnp.dot(block[...], weight[...], preferred_element_type=F32).astype(BF16)
        out[2 * i] = product[:per_chunk]
        out[2 * i + 1] = product[per_chunk:]


def keys_kernel(a, b, cosine, sine_v, out):
    total = (a[...].astype(F32) + b[...].astype(F32)).astype(BF16).astype(F32)
    out[...] = rotate(total, cosine[...], sine_v[...]).astype(BF16)


def attention_kernel(heads, base, own, got, cosine, sine_v, *refs):
    keys, values, out, queries = refs[:4], refs[4:8], refs[8], refs[9]
    per_chunk = own.shape[0]
    for h in range(heads):
        cols = slice(h * HD, (h + 1) * HD)
        total = own[:, cols].astype(F32) + got[:, cols].astype(F32)
        queries[h * per_chunk : (h + 1) * per_chunk, :] = rotate(
            total, cosine[...], sine_v[...]
        ).astype(BF16)
    query = queries[...]
    rows = heads * per_chunk
    row_pos = base[8] + lax.broadcasted_iota(jnp.int32, (rows, HD), 0) % per_chunk
    lane = lax.broadcasted_iota(jnp.int32, (rows, HD), 1)
    score_scale = 1.0 / math.sqrt(HD)
    totals = jnp.zeros((rows, 1), F32)
    mixed = jnp.zeros((rows, HD), F32)
    for s in range(4):
        scores = (
            lax.dot_general(
                query, keys[s][...], (((1,), (1,)), ((), ())), preferred_element_type=F32
            )
            * score_scale
        )
        causal = jnp.concatenate(
            [base[2 * s] + lane <= row_pos, base[2 * s + 1] + lane <= row_pos], 1
        )
        weights = jnp.where(causal, jnp.exp(jnp.where(causal, scores, 0.0)), 0.0)
        totals += jnp.sum(weights, 1, keepdims=True)
        mixed += jnp.dot(weights.astype(BF16), values[s][...], preferred_element_type=F32)
    attended = (mixed / totals).astype(BF16)
    for h in range(heads):
        block = attended[h * per_chunk : (h + 1) * per_chunk]
        for c in range(out.shape[0]):
            out[c, :, h * HD : (h + 1) * HD] = block


def chip_kernel(kept, got, *outs):
    rows = outs[0].shape[0]
    for s, out in enumerate(outs):
        part = slice(s * rows, (s + 1) * rows)
        out[...] = (kept[part, :].astype(F32) + got[part, :].astype(F32)).astype(BF16)


def call(kernel, outs, args, scratch=(), scalars=0):
    return pl.pallas_call(
        kernel,
        out_shape=[jax.ShapeDtypeStruct(s, BF16) for s in outs],
        in_specs=[SMEM] * scalars + [VMEM] * (len(args) - scalars),
        out_specs=[VMEM] * len(outs),
        scratch_shapes=list(scratch),
        compiler_params=PARAMS,
    )(*args)


def shards(tokens, w_query, w_keyval, w_output):
    zl = lax.axis_index("zl")
    core = lax.axis_index("core")
    y = lax.axis_index("y")
    x = lax.axis_index("x")
    per_row, features = tokens.shape
    half = per_row * Z_LO
    total = half * 2
    per_chunk = total // (Y * X)
    quarter = total // X
    width = w_query.shape[1]
    heads = width // HD

    mine = [tokens] + [partner(tokens, "zl", s) for s in (1, 2, 3)]
    others = [partner(block, "core", 1) for block in mine]
    everyone = mine + others
    kv_moves = [(e, 2 * e if e < 4 else 2 * (e - 4) + 1) for e in range(8)]
    w_kv = lax.ppermute(w_keyval, ROW, kv_moves)

    def block_start(chip_step, side):
        return (2 * (zl ^ chip_step) + side) * per_row

    starts = []
    for s in range(X):
        j = x ^ s
        for b in range(2):
            starts.append(block_start(2 * (j % 2) + b, j // 2))
    chunk = y * X + x
    row_block = chunk // 2
    row_start = block_start(row_block % 4, (row_block // 4) ^ core) + (chunk % 2) * per_chunk
    base = jnp.stack([*starts, row_start]).astype(jnp.int32)
    pick = jnp.stack([(x ^ s) ^ (2 * core) for s in range(X)]).astype(jnp.int32)
    query_cos, query_sin = tables((row_start + jnp.arange(per_chunk)).astype(F32), HD)
    key_pos = jnp.concatenate([starts[0] + jnp.arange(per_row), starts[1] + jnp.arange(per_row)])
    key_cos, key_sin = tables(key_pos.astype(F32), HD)
    key_cos = jnp.where(core == 0, key_cos, 1.0)
    key_sin = jnp.where(core == 0, key_sin, 0.0)

    kv_parts = call(
        kv_kernel,
        [(quarter, HD)] * 4,
        [pick, *everyone, w_kv],
        [pltpu.VMEM((4, quarter, HD), BF16)],
        scalars=1,
    )
    (query_parts,) = call(query_kernel, [(Y * X, per_chunk, width)], [*everyone, w_query])
    query_parts = lax.all_to_all(query_parts, PLANE, 0, 0, tiled=True)

    def add(blocks):
        return functools.reduce(jnp.add, [b.astype(F32) for b in blocks]).astype(BF16)

    kv_x = add([kv_parts[0]] + [partner(kv_parts[s], "x", s) for s in (1, 2, 3)])
    kv_y = add([kv_x] + [partner(kv_x, "y", s) for s in (1, 2, 3)])
    (kv_done,) = call(
        keys_kernel, [(quarter, HD)], [kv_y, partner(kv_y, "zh", 1), key_cos, key_sin]
    )
    kv_other = partner(kv_done, "core", 1)
    keys = jnp.where(core == 0, kv_done, kv_other)
    values = jnp.where(core == 0, kv_other, kv_done)
    both = jnp.stack([keys, values])
    both = [both] + [partner(both, "x", s) for s in (1, 2, 3)]

    own = jnp.sum(query_parts.astype(F32), 0).astype(BF16)
    got = partner(own, "zh", 1)
    (attended,) = call(
        functools.partial(attention_kernel, heads),
        [(Y * X, per_chunk, width)],
        [base, own, got, query_cos, query_sin, *[b[0] for b in both], *[b[1] for b in both]],
        [pltpu.VMEM((heads * per_chunk, HD), BF16)],
        scalars=1,
    )
    attended = lax.all_to_all(attended, PLANE, 0, 0, tiled=True).reshape(total, width)

    sent = jnp.dot(attended[half:], w_output, preferred_element_type=F32).astype(BF16)
    kept = jnp.dot(attended[:half], w_output, preferred_element_type=F32).astype(BF16)
    chip = call(chip_kernel, [(per_row, features)] * 4, [kept, partner(sent, "core", 1)])
    return add([chip[0]] + [partner(chip[s], "zl", s) for s in (3, 2, 1)])


def solution(mesh):
    fine = Mesh(
        mesh.devices.reshape(Z_LO, CORE, Z_HI, Y, X), ("zl", "core", "zh", "y", "x")
    )
    return jax.shard_map(
        shards,
        mesh=fine,
        in_specs=(P(ROW, COL), P(COL, ROW), P(COL, ROW), P(ROW, COL)),
        out_specs=P(ROW, COL),
        check_vma=False,
    )
```

```python
import functools
import math

import jax
import jax.numpy as jnp
from jax import lax
from jax.experimental import pallas as pl
from jax.experimental.pallas import tpu as pltpu
from jax.sharding import Mesh
from jax.sharding import PartitionSpec as P

HD = 128
Z_LO, CORE, Z_HI, Y, X = 4, 2, 2, 4, 4
ROW = ("zl", "core")
COL = ("zh", "y", "x")
PLANE = ("y", "x")
BF16 = jnp.bfloat16
F32 = jnp.float32
VMEM = pl.BlockSpec(memory_space=pltpu.VMEM)
SMEM = pl.BlockSpec(memory_space=pltpu.SMEM)
PARAMS = pltpu.CompilerParams(vmem_limit_bytes=32 * 1024 * 1024)


def tables(positions, width):
    half_width = width // 2
    frequency = 500000.0 ** (-(jnp.arange(half_width).astype(F32) * 2.0 / width))
    angle_v = positions[:, None] * frequency[None, :]
    cosine, sine_v = jnp.cos(angle_v), jnp.sin(angle_v)
    return jnp.concatenate([cosine, cosine], 1), jnp.concatenate([-sine_v, sine_v], 1)


def rotate(values_in, cosine, sine_v):
    return values_in * cosine + pltpu.roll(values_in, HD // 2, 1) * sine_v


def partner(block, axis, step):
    size = {"zl": Z_LO, "core": CORE, "zh": Z_HI, "y": Y, "x": X}[axis]
    return lax.ppermute(block, axis, [(i, i ^ step) for i in range(size)])


def projection_kernel(*refs):
    blocks, w_query, w_kv, out = refs[:8], refs[8], refs[9], refs[10]
    per_chunk = out.shape[1]
    width = w_query.shape[1]
    for i, block in enumerate(blocks):
        query = jnp.dot(block[...], w_query[...], preferred_element_type=F32).astype(BF16)
        keyval = jnp.dot(block[...], w_kv[...], preferred_element_type=F32).astype(BF16)
        for b in range(2):
            part = slice(b * per_chunk, (b + 1) * per_chunk)
            out[2 * i + b, :, :width] = query[part]
            out[2 * i + b, :, width:] = keyval[part]


def sums_kernel(parts, query, keyval):
    width = query.shape[1]
    total = parts[0].astype(F32)
    for c in range(1, parts.shape[0]):
        total += parts[c].astype(F32)
    query[...] = total[:, :width].astype(BF16)
    keyval[...] = total[:, width:].astype(BF16)


def keys_kernel(a, b, cosine, sine_v, out):
    total = (a[...].astype(F32) + b[...].astype(F32)).astype(BF16).astype(F32)
    block = rotate(total, cosine[...], sine_v[...]).astype(BF16)
    for c in range(out.shape[0]):
        out[c] = block


def attention_kernel(heads, base, own, got, cosine, sine_v, kv_own, kv_other, out, queries, pair):
    per_chunk = own.shape[0]
    half = kv_own.shape[0] // 2
    for side in range(2):
        pair[0, side * half : (side + 1) * half, :] = kv_own[side * half : (side + 1) * half, :]
        pair[1, side * half : (side + 1) * half, :] = kv_other[
            (1 - side) * half : (2 - side) * half, :
        ]
    for h in range(heads):
        cols = slice(h * HD, (h + 1) * HD)
        total = own[:, cols].astype(F32) + got[:, cols].astype(F32)
        queries[h * per_chunk : (h + 1) * per_chunk, :] = rotate(
            total, cosine[...], sine_v[...]
        ).astype(BF16)
    query = queries[...]
    core = base[9]
    rows = heads * per_chunk
    row_pos = base[8] + lax.broadcasted_iota(jnp.int32, (rows, HD), 0) % per_chunk
    lane = lax.broadcasted_iota(jnp.int32, (rows, HD), 1)
    score_scale = 1.0 / math.sqrt(HD)
    totals = jnp.zeros((rows, 1), F32)
    mixed = jnp.zeros((rows, HD), F32)
    for s in range(4):
        part = slice(s * 2 * HD, (s + 1) * 2 * HD)
        keys, values = pair[core, part, :], pair[1 - core, part, :]
        scores = (
            lax.dot_general(query, keys, (((1,), (1,)), ((), ())), preferred_element_type=F32)
            * score_scale
        )
        causal = jnp.concatenate(
            [base[2 * s] + lane <= row_pos, base[2 * s + 1] + lane <= row_pos], 1
        )
        weights = jnp.where(causal, jnp.exp(jnp.where(causal, scores, 0.0)), 0.0)
        totals += jnp.sum(weights, 1, keepdims=True)
        mixed += jnp.dot(weights.astype(BF16), values, preferred_element_type=F32)
    attended = (mixed / totals).astype(BF16)
    for h in range(heads):
        block = attended[h * per_chunk : (h + 1) * per_chunk]
        for c in range(out.shape[0]):
            out[c, :, h * HD : (h + 1) * HD] = block


def chip_kernel(kept, got, *outs):
    rows = outs[0].shape[0]
    for s, out in enumerate(outs):
        part = slice(s * rows, (s + 1) * rows)
        out[...] = (kept[part, :].astype(F32) + got[part, :].astype(F32)).astype(BF16)


def call(kernel, outs, args, scratch=(), scalars=0):
    return pl.pallas_call(
        kernel,
        out_shape=[jax.ShapeDtypeStruct(s, BF16) for s in outs],
        in_specs=[SMEM] * scalars + [VMEM] * (len(args) - scalars),
        out_specs=[VMEM] * len(outs),
        scratch_shapes=list(scratch),
        compiler_params=PARAMS,
    )(*args)


def shards(tokens, w_query, w_keyval, w_output):
    zl = lax.axis_index("zl")
    core = lax.axis_index("core")
    y = lax.axis_index("y")
    x = lax.axis_index("x")
    per_row, features = tokens.shape
    half = per_row * Z_LO
    total = half * 2
    per_chunk = total // (Y * X)
    width = w_query.shape[1]
    heads = width // HD

    mine = [tokens] + [partner(tokens, "zl", s) for s in (1, 2, 3)]
    others = [partner(block, "core", 1) for block in mine]
    everyone = mine + others
    kv_moves = [(e, 2 * e if e < 4 else 2 * (e - 4) + 1) for e in range(8)]
    w_kv = lax.ppermute(w_keyval, ROW, kv_moves)

    def block_start(index):
        return (((zl ^ (index & 3)) << 1) + ((index >> 2) ^ core)) * per_row

    chunk = y * X + x
    row_start = block_start(chunk >> 1) + (chunk & 1) * per_chunk
    base = jnp.stack([*[block_start(i) for i in range(8)], row_start, core]).astype(jnp.int32)
    cosine, sine_v = tables((row_start + jnp.arange(per_chunk)).astype(F32), HD)
    key_cos = jnp.where(core == 0, cosine, 1.0)
    key_sin = jnp.where(core == 0, sine_v, 0.0)

    (parts,) = call(
        projection_kernel, [(Y * X, per_chunk, width + HD)], [*everyone, w_query, w_kv]
    )
    parts = lax.all_to_all(parts, PLANE, 0, 0, tiled=True)
    query, kv = call(sums_kernel, [(per_chunk, width), (per_chunk, HD)], [parts])
    (kv_block,) = call(
        keys_kernel, [(Y * X, per_chunk, HD)], [kv, partner(kv, "zh", 1), key_cos, key_sin]
    )
    kv_own = lax.all_to_all(kv_block, PLANE, 0, 0, tiled=True).reshape(total, HD)
    kv_other = partner(kv_own, "core", 1)
    query_got = partner(query, "zh", 1)
    (attended,) = call(
        functools.partial(attention_kernel, heads),
        [(Y * X, per_chunk, width)],
        [base, query, query_got, cosine, sine_v, kv_own, kv_other],
        [pltpu.VMEM((heads * per_chunk, HD), BF16), pltpu.VMEM((2, total, HD), BF16)],
        scalars=1,
    )
    attended = lax.all_to_all(attended, PLANE, 0, 0, tiled=True).reshape(total, width)

    sent = jnp.dot(attended[half:], w_output, preferred_element_type=F32).astype(BF16)
    kept = jnp.dot(attended[:half], w_output, preferred_element_type=F32).astype(BF16)
    chip = call(chip_kernel, [(per_row, features)] * 4, [kept, partner(sent, "core", 1)])
    blocks = [chip[0]] + [partner(chip[s], "zl", s) for s in (3, 2, 1)]
    return functools.reduce(jnp.add, [b.astype(F32) for b in blocks]).astype(BF16)


def solution(mesh):
    fine = Mesh(
        mesh.devices.reshape(Z_LO, CORE, Z_HI, Y, X), ("zl", "core", "zh", "y", "x")
    )
    return jax.shard_map(
        shards,
        mesh=fine,
        in_specs=(P(ROW, COL), P(COL, ROW), P(COL, ROW), P(ROW, COL)),
        out_specs=P(ROW, COL),
        check_vma=False,
    )
```

```python
import functools
import math

import jax
import jax.numpy as jnp
from jax import lax
from jax.experimental import pallas as pl
from jax.experimental.pallas import tpu as pltpu
from jax.sharding import Mesh
from jax.sharding import PartitionSpec as P

HD = 128
Z_LO, CORE, Z_HI, Y, X = 4, 2, 2, 4, 4
ROW = ("zl", "core")
COL = ("zh", "y", "x")
PLANE = ("y", "x")
BF16 = jnp.bfloat16
F32 = jnp.float32
VMEM = pl.BlockSpec(memory_space=pltpu.VMEM)
SMEM = pl.BlockSpec(memory_space=pltpu.SMEM)
HBM = pl.BlockSpec(memory_space=pltpu.HBM)


def tables(positions, width):
    half_width = width // 2
    frequency = 500000.0 ** (-(jnp.arange(half_width).astype(F32) * 2.0 / width))
    angle_v = positions[:, None] * frequency[None, :]
    cosine, sine_v = jnp.cos(angle_v), jnp.sin(angle_v)
    return jnp.concatenate([cosine, cosine], 1), jnp.concatenate([-sine_v, sine_v], 1)


def rotate(values_in, cosine, sine_v):
    return values_in * cosine + pltpu.roll(values_in, HD // 2, 1) * sine_v


def partner(block, axis, step):
    size = {"zl": Z_LO, "core": CORE, "zh": Z_HI, "y": Y, "x": X}[axis]
    return lax.ppermute(block, axis, [(i, i ^ step) for i in range(size)])


def projection_kernel(place, own, *refs):
    blocks, w_hbm, w_kv = refs[:7], refs[7], refs[8]
    outs_x, outs_y = refs[9:13], refs[13:17]
    chunks, w_query, first, sems = refs[17:]
    copies = [pltpu.make_async_copy(own, first, sems.at[4])]
    rows = w_query.shape[0] // 4
    for i in range(4):
        part = pl.ds(i * rows, rows)
        copies.append(pltpu.make_async_copy(w_hbm.at[part], w_query.at[part], sems.at[i]))
    for copy in copies:
        copy.start()
    for copy in copies:
        copy.wait()
    size = chunks.shape[1]
    width = w_query.shape[1]
    for i, block in enumerate([first, *blocks]):
        query = jnp.dot(block[...], w_query[...], preferred_element_type=F32).astype(BF16)
        keyval = jnp.dot(block[...], w_kv[...], preferred_element_type=F32).astype(BF16)
        for b in range(2):
            part = slice(b * size, (b + 1) * size)
            chunks[2 * i + b, :, :width] = query[part]
            chunks[2 * i + b, :, width:] = keyval[part]
    x, y = place[0], place[1]
    for s in range(4):
        for j in range(4):
            outs_x[s][j] = chunks[4 * j + (x ^ s), : size // 2, :]
            outs_y[s][j] = chunks[4 * (y ^ s) + j, size // 2 :, :]


def halve_kernel(place, a, b, c, d, own, *outs):
    for t, out in enumerate([own, *outs]):
        j = place[0] ^ t
        total = a[j].astype(F32) + b[j].astype(F32) + c[j].astype(F32) + d[j].astype(F32)
        out[...] = total.astype(out.dtype)


def join_kernel(*refs):
    out = refs[8]
    rows = out.shape[0] // 2
    for side in range(2):
        total = functools.reduce(
            jnp.add, [ref[...].astype(F32) for ref in refs[4 * side : 4 * side + 4]]
        )
        out[side * rows : (side + 1) * rows, :] = total.astype(BF16)


def keys_kernel(a, b, cosine, sine_v, out):
    width = a.shape[1] - HD
    total = a[:, width:].astype(F32) + b[:, width:].astype(F32)
    total = total.astype(BF16).astype(F32)
    block = rotate(total, cosine[...], sine_v[...]).astype(BF16)
    for c in range(out.shape[0]):
        out[c] = block


def attention_kernel(
    heads, base, own, got, cosine, sine_v, kv_own, kv_other, low, high, queries, pair
):
    per_chunk = own.shape[0]
    half = kv_own.shape[0] // 2
    for side in range(2):
        pair[0, side * half : (side + 1) * half, :] = kv_own[side * half : (side + 1) * half, :]
        pair[1, side * half : (side + 1) * half, :] = kv_other[
            (1 - side) * half : (2 - side) * half, :
        ]
    for h in range(heads):
        cols = slice(h * HD, (h + 1) * HD)
        total = own[:, cols].astype(F32) + got[:, cols].astype(F32)
        queries[h * per_chunk : (h + 1) * per_chunk, :] = rotate(
            total, cosine[...], sine_v[...]
        ).astype(BF16)
    query = queries[...]
    core = base[9]
    rows = heads * per_chunk
    row_pos = base[8] + lax.broadcasted_iota(jnp.int32, (rows, HD), 0) % per_chunk
    lane = lax.broadcasted_iota(jnp.int32, (rows, HD), 1)
    score_scale = 1.0 / math.sqrt(HD)
    totals = jnp.zeros((rows, 1), F32)
    mixed = jnp.zeros((rows, HD), F32)
    for s in range(4):
        part = slice(s * 2 * HD, (s + 1) * 2 * HD)
        keys, values = pair[core, part, :], pair[1 - core, part, :]
        scores = (
            lax.dot_general(query, keys, (((1,), (1,)), ((), ())), preferred_element_type=F32)
            * score_scale
        )
        causal = jnp.concatenate(
            [base[2 * s] + lane <= row_pos, base[2 * s + 1] + lane <= row_pos], 1
        )
        weights = jnp.where(causal, jnp.exp(jnp.where(causal, scores, 0.0)), 0.0)
        totals += jnp.sum(weights, 1, keepdims=True)
        mixed += jnp.dot(weights.astype(BF16), values, preferred_element_type=F32)
    attended = (mixed / totals).astype(BF16)
    cut = per_chunk // 2
    for h in range(heads):
        cols = slice(h * HD, (h + 1) * HD)
        low[:, cols] = attended[h * per_chunk : h * per_chunk + cut]
        high[:, cols] = attended[h * per_chunk + cut : (h + 1) * per_chunk]


def stack_kernel(*refs):
    for s, ref in enumerate(refs[:4]):
        refs[4][s] = ref[...]


def output_kernel(place, *refs):
    by_y, by_x, weight, kept, sent, chunks = refs[:4], refs[4:8], *refs[8:]
    x, y = place[0], place[1]
    rows, width = by_y[0].shape[1:]
    for side, arrays in enumerate((by_y, by_x)):
        for t, array in enumerate(arrays):
            block = array[...].reshape(4 * rows, width)
            product = jnp.dot(block, weight[...], preferred_element_type=F32).astype(BF16)
            for s in range(4):
                k = 4 * (y ^ t) + (x ^ s) if side == 0 else 4 * (y ^ s) + (x ^ t)
                chunks[k, side * rows : (side + 1) * rows, :] = product[s * rows : (s + 1) * rows]
    half = kept.shape[0]
    kept[...] = chunks[:half]
    sent[...] = chunks[half:]


def chip_kernel(kept, got, *outs):
    rows = outs[0].shape[0]
    for s, out in enumerate(outs):
        part = slice(s * rows, (s + 1) * rows)
        out[...] = (kept[part, :].astype(F32) + got[part, :].astype(F32)).astype(BF16)


def call(kernel, outs, args, specs=(), scratch=()):
    specs = list(specs) + [VMEM] * (len(args) - len(specs))
    return pl.pallas_call(
        kernel,
        out_shape=[
            s if isinstance(s, jax.ShapeDtypeStruct) else jax.ShapeDtypeStruct(s, BF16)
            for s in outs
        ],
        in_specs=specs,
        out_specs=[VMEM] * len(outs),
        scratch_shapes=list(scratch),
        compiler_params=pltpu.CompilerParams(vmem_limit_bytes=32 * 1024 * 1024),
    )(*args)


def shards(tokens, w_query, w_keyval, w_output):
    zl = lax.axis_index("zl")
    core = lax.axis_index("core")
    y = lax.axis_index("y")
    x = lax.axis_index("x")
    per_row, features = tokens.shape
    half = per_row * Z_LO
    total = half * 2
    per_chunk = total // (Y * X)
    cut = per_chunk // 2
    width = w_query.shape[1]
    heads = width // HD
    both = width + HD

    mine = [tokens] + [partner(tokens, "zl", s) for s in (1, 2, 3)]
    others = [partner(block, "core", 1) for block in mine]
    kv_moves = [(e, 2 * e if e < 4 else 2 * (e - 4) + 1) for e in range(8)]
    w_kv = lax.ppermute(w_keyval, ROW, kv_moves)

    def block_start(index):
        return (((zl ^ (index & 3)) << 1) + ((index >> 2) ^ core)) * per_row

    chunk = y * X + x
    row_start = block_start(chunk >> 1) + (chunk & 1) * per_chunk
    base = jnp.stack([*[block_start(i) for i in range(8)], row_start, core]).astype(jnp.int32)
    cosine, sine_v = tables((row_start + jnp.arange(per_chunk)).astype(F32), HD)
    key_cos = jnp.where(core == 0, cosine, 1.0)
    key_sin = jnp.where(core == 0, sine_v, 0.0)
    place_xy = jnp.stack([x, y]).astype(jnp.int32)
    place_yx = jnp.stack([y, x]).astype(jnp.int32)

    parts = call(
        projection_kernel,
        [(4, cut, both)] * 8,
        [place_xy, tokens, *mine[1:], *others, w_query, w_kv],
        [SMEM, HBM, *[VMEM] * 7, HBM],
        [
            pltpu.VMEM((Y * X, per_chunk, both), BF16),
            pltpu.VMEM(w_query.shape, BF16),
            pltpu.VMEM(tokens.shape, BF16),
            pltpu.SemaphoreType.DMA((5,)),
        ],
    )
    summed = []
    for place, first, second, pieces in (
        (place_yx, "x", "y", parts[:4]),
        (place_xy, "y", "x", parts[4:]),
    ):
        got = [partner(pieces[s], first, s) for s in (1, 2, 3)]
        own, *sends = call(
            halve_kernel,
            [jax.ShapeDtypeStruct((cut, both), F32), *[(cut, both)] * 3],
            [place, pieces[0], *got],
            [SMEM],
        )
        summed += [own] + [partner(sends[t - 1], second, t) for t in (1, 2, 3)]
    (own,) = call(join_kernel, [(per_chunk, both)], summed)
    got = partner(own, "zh", 1)

    (kv_block,) = call(keys_kernel, [(Y * X, per_chunk, HD)], [own, got, key_cos, key_sin])
    kv_own = lax.all_to_all(kv_block, PLANE, 0, 0, tiled=True).reshape(total, HD)
    kv_other = partner(kv_own, "core", 1)
    low, high = call(
        functools.partial(attention_kernel, heads),
        [(cut, width)] * 2,
        [base, own, got, cosine, sine_v, kv_own, kv_other],
        [SMEM],
        [pltpu.VMEM((heads * per_chunk, HD), BF16), pltpu.VMEM((2, total, HD), BF16)],
    )

    gathered = []
    for first, second, block in (("x", "y", low), ("y", "x", high)):
        (line,) = call(
            stack_kernel,
            [(4, cut, width)],
            [block] + [partner(block, first, s) for s in (1, 2, 3)],
        )
        gathered += [line] + [partner(line, second, t) for t in (1, 2, 3)]
    kept, sent = call(
        output_kernel,
        [(Y * X // 2, per_chunk, features)] * 2,
        [place_xy, *gathered, w_output],
        [SMEM],
        [pltpu.VMEM((Y * X, per_chunk, features), BF16)],
    )
    kept, sent = kept.reshape(half, features), sent.reshape(half, features)
    chip = call(chip_kernel, [(per_row, features)] * 4, [kept, partner(sent, "core", 1)])
    blocks = [chip[0]] + [partner(chip[s], "zl", s) for s in (3, 2, 1)]
    return functools.reduce(jnp.add, [b.astype(F32) for b in blocks]).astype(BF16)


def solution(mesh):
    fine = Mesh(
        mesh.devices.reshape(Z_LO, CORE, Z_HI, Y, X), ("zl", "core", "zh", "y", "x")
    )
    return jax.shard_map(
        shards,
        mesh=fine,
        in_specs=(P(ROW, COL), P(COL, ROW), P(COL, ROW), P(ROW, COL)),
        out_specs=P(ROW, COL),
        check_vma=False,
    )
```

```python
import functools
import math

import jax
import jax.numpy as jnp
from jax import lax
from jax.experimental import pallas as pl
from jax.experimental.pallas import tpu as pltpu
from jax.sharding import Mesh
from jax.sharding import PartitionSpec as P

HD = 128
Z_LO, CORE, Z_HI, Y, X = 4, 2, 2, 4, 4
ROW = ("zl", "core")
COL = ("zh", "y", "x")
PLANE = ("y", "x")
BF16 = jnp.bfloat16
F32 = jnp.float32
VMEM = pl.BlockSpec(memory_space=pltpu.VMEM)
SMEM = pl.BlockSpec(memory_space=pltpu.SMEM)


def tables(positions, width):
    half_width = width // 2
    frequency = 500000.0 ** (-(jnp.arange(half_width).astype(F32) * 2.0 / width))
    angle_v = positions[:, None] * frequency[None, :]
    cosine, sine_v = jnp.cos(angle_v), jnp.sin(angle_v)
    return jnp.concatenate([cosine, cosine], 1), jnp.concatenate([-sine_v, sine_v], 1)


def rotate(values_in, cosine, sine_v):
    return values_in * cosine + pltpu.roll(values_in, HD // 2, 1) * sine_v


def partner(block, axis, step):
    size = {"zl": Z_LO, "core": CORE, "zh": Z_HI, "y": Y, "x": X}[axis]
    return lax.ppermute(block, axis, [(i, i ^ step) for i in range(size)])


def project(block, w_query, w_kv, chunks, k):
    size = chunks.shape[1]
    width = w_query.shape[1]
    query = jnp.dot(block[...], w_query[...], preferred_element_type=F32).astype(BF16)
    keyval = jnp.dot(block[...], w_kv[...], preferred_element_type=F32).astype(BF16)
    for b in range(2):
        part = slice(b * size, (b + 1) * size)
        chunks[k + b, :, :width] = query[part]
        chunks[k + b, :, width:] = keyval[part]


def early_kernel(*refs):
    blocks, w_query, w_kv, out = refs[:2], *refs[2:]
    for i, block in enumerate(blocks):
        project(block, w_query, w_kv, out, 2 * i)


def late_kernel(place, *refs):
    blocks, w_query, w_kv, early = refs[:6], *refs[6:9]
    outs_x, outs_y, chunks = refs[9:13], refs[13:17], refs[17]
    for side in range(2):
        chunks[8 * side] = early[2 * side]
        chunks[8 * side + 1] = early[2 * side + 1]
        for i in range(3):
            project(blocks[3 * side + i], w_query, w_kv, chunks, 8 * side + 2 * i + 2)
    cut = chunks.shape[1] // 2
    x, y = place[0], place[1]
    for s in range(4):
        for j in range(4):
            outs_x[s][j] = chunks[4 * j + (x ^ s), :cut, :]
            outs_y[s][j] = chunks[4 * (y ^ s) + j, cut:, :]


def halve_kernel(place, *refs):
    for side in range(2):
        a, b, c, d = refs[4 * side : 4 * side + 4]
        for t in range(4):
            out = refs[8 + 4 * side + t]
            j = place[1 - side] ^ t
            total = a[j].astype(F32) + b[j].astype(F32) + c[j].astype(F32) + d[j].astype(F32)
            out[...] = total.astype(out.dtype)


def join_kernel(*refs):
    query, keyval = refs[8:]
    rows, width = query.shape[0] // 2, query.shape[1]
    for side in range(2):
        total = functools.reduce(
            jnp.add, [ref[...].astype(F32) for ref in refs[4 * side : 4 * side + 4]]
        ).astype(BF16)
        query[side * rows : (side + 1) * rows, :] = total[:, :width]
        keyval[side * rows : (side + 1) * rows, :] = total[:, width:]


def keys_kernel(a, b, cosine, sine_v, out):
    total = (a[...].astype(F32) + b[...].astype(F32)).astype(BF16).astype(F32)
    block = rotate(total, cosine[...], sine_v[...]).astype(BF16)
    for c in range(out.shape[0]):
        out[c] = block


def attention_kernel(
    heads, base, own, got, cosine, sine_v, kv_own, kv_other, low, high, queries, pair
):
    per_chunk = own.shape[0]
    pair[0] = kv_own[...]
    for s in range(4):
        part = slice(s * 2 * HD, (s + 1) * 2 * HD)
        pair[1, part, :] = kv_other[(s ^ 1) * 2 * HD : ((s ^ 1) + 1) * 2 * HD, :]
    for h in range(heads):
        cols = slice(h * HD, (h + 1) * HD)
        total = own[:, cols].astype(F32) + got[:, cols].astype(F32)
        queries[h * per_chunk : (h + 1) * per_chunk, :] = rotate(
            total, cosine[...], sine_v[...]
        ).astype(BF16)
    query = queries[...]
    core = base[9]
    rows = heads * per_chunk
    row_pos = base[8] + lax.broadcasted_iota(jnp.int32, (rows, HD), 0) % per_chunk
    lane = lax.broadcasted_iota(jnp.int32, (rows, HD), 1)
    score_scale = 1.0 / math.sqrt(HD)
    totals = jnp.zeros((rows, 1), F32)
    mixed = jnp.zeros((rows, HD), F32)
    for s in range(4):
        part = slice(s * 2 * HD, (s + 1) * 2 * HD)
        keys, values = pair[core, part, :], pair[1 - core, part, :]
        scores = (
            lax.dot_general(query, keys, (((1,), (1,)), ((), ())), preferred_element_type=F32)
            * score_scale
        )
        causal = jnp.concatenate(
            [base[2 * s] + lane <= row_pos, base[2 * s + 1] + lane <= row_pos], 1
        )
        weights = jnp.where(causal, jnp.exp(jnp.where(causal, scores, 0.0)), 0.0)
        totals += jnp.sum(weights, 1, keepdims=True)
        mixed += jnp.dot(weights.astype(BF16), values, preferred_element_type=F32)
    attended = (mixed / totals).astype(BF16)
    cut = per_chunk // 2
    for h in range(heads):
        cols = slice(h * HD, (h + 1) * HD)
        low[:, cols] = attended[h * per_chunk : h * per_chunk + cut]
        high[:, cols] = attended[h * per_chunk + cut : (h + 1) * per_chunk]


def stack_kernel(*refs):
    for side in range(2):
        for s in range(4):
            refs[8 + side][s] = refs[4 * side + s][...]


def output_kernel(place, *refs):
    by_y, by_x, weight, kept, sent, chunks = refs[:4], refs[4:8], *refs[8:]
    x, y = place[0], place[1]
    rows, width = by_y[0].shape[1:]
    for side, arrays in enumerate((by_y, by_x)):
        for t, array in enumerate(arrays):
            block = array[...].reshape(4 * rows, width)
            product = jnp.dot(block, weight[...], preferred_element_type=F32).astype(BF16)
            for s in range(4):
                k = 4 * (y ^ t) + (x ^ s) if side == 0 else 4 * (y ^ s) + (x ^ t)
                chunks[k, side * rows : (side + 1) * rows, :] = product[s * rows : (s + 1) * rows]
    half = kept.shape[0]
    kept[...] = chunks[:half]
    sent[...] = chunks[half:]


def chip_kernel(kept, got, *outs):
    rows = outs[0].shape[0]
    for s, out in enumerate(outs):
        part = slice(s * rows, (s + 1) * rows)
        out[...] = (kept[part, :].astype(F32) + got[part, :].astype(F32)).astype(BF16)


def call(kernel, outs, args, specs=(), scratch=()):
    specs = list(specs) + [VMEM] * (len(args) - len(specs))
    return pl.pallas_call(
        kernel,
        out_shape=[
            s if isinstance(s, jax.ShapeDtypeStruct) else jax.ShapeDtypeStruct(s, BF16)
            for s in outs
        ],
        in_specs=specs,
        out_specs=[VMEM] * len(outs),
        scratch_shapes=list(scratch),
        compiler_params=pltpu.CompilerParams(vmem_limit_bytes=32 * 1024 * 1024),
    )(*args)


def shards(tokens, w_query, w_keyval, w_output):
    zl = lax.axis_index("zl")
    core = lax.axis_index("core")
    y = lax.axis_index("y")
    x = lax.axis_index("x")
    per_row, features = tokens.shape
    half = per_row * Z_LO
    total = half * 2
    per_chunk = total // (Y * X)
    cut = per_chunk // 2
    width = w_query.shape[1]
    heads = width // HD
    both = width + HD

    mine = [tokens] + [partner(tokens, "zl", s) for s in (1, 2, 3)]

    def block_start(chip, side, index):
        return (((chip ^ (index & 3)) << 1) + ((index >> 2) ^ side)) * per_row

    chunk = y * X + x
    offset = (chunk & 1) * per_chunk
    source_chip, source_core = (zl >> 1) + 2 * core, zl & 1
    row_start = block_start(zl, core, chunk >> 1) + offset
    key_start = block_start(source_chip, source_core, chunk >> 1) + offset
    starts = [block_start(source_chip, source_core, i) for i in range(8)]
    base = jnp.stack([*starts, row_start, core]).astype(jnp.int32)
    steps = jnp.arange(per_chunk)
    cosine, sine_v = tables((row_start + steps).astype(F32), HD)
    key_cos, key_sin = tables((key_start + steps).astype(F32), HD)
    key_cos = jnp.where(core == 0, key_cos, 1.0)
    key_sin = jnp.where(core == 0, key_sin, 0.0)
    place = jnp.stack([x, y]).astype(jnp.int32)

    near = partner(tokens, "core", 1)
    (early,) = call(early_kernel, [(4, per_chunk, both)], [tokens, near, w_query, w_keyval])
    *far, early = lax.optimization_barrier((*mine[1:], early))
    parts = call(
        late_kernel,
        [(4, cut, both)] * 8,
        [place, *far, *[partner(block, "core", 1) for block in far], w_query, w_keyval, early],
        [SMEM],
        [pltpu.VMEM((Y * X, per_chunk, both), BF16)],
    )
    got_x = [partner(parts[s], "x", s) for s in (1, 2, 3)]
    got_y = [partner(parts[4 + s], "y", s) for s in (1, 2, 3)]
    kept_f32 = jax.ShapeDtypeStruct((cut, both), F32)
    halves = call(
        halve_kernel,
        [kept_f32, *[(cut, both)] * 3] * 2,
        [place, parts[0], *got_x, parts[4], *got_y],
        [SMEM],
    )
    got_y = [partner(halves[t], "y", t) for t in (1, 2, 3)]
    got_x = [partner(halves[4 + t], "x", t) for t in (1, 2, 3)]
    own, kv = call(
        join_kernel,
        [(per_chunk, width), (per_chunk, HD)],
        [halves[0], *got_y, halves[4], *got_x],
    )
    got = partner(own, "zh", 1)

    moves = [(e, 2 * (e % 4) + e // 4) for e in range(8)]
    here = lax.ppermute(kv, ROW, moves)
    across = lax.ppermute(
        kv, (*ROW, "zh"), [(2 * e + h, 2 * r + 1 - h) for e, r in moves for h in range(2)]
    )
    (kv_block,) = call(keys_kernel, [(Y * X, per_chunk, HD)], [here, across, key_cos, key_sin])
    kv_own = lax.all_to_all(kv_block, PLANE, 0, 0, tiled=True).reshape(total, HD)
    kv_other = partner(kv_own, "core", 1)
    low, high = call(
        functools.partial(attention_kernel, heads),
        [(cut, width)] * 2,
        [base, own, got, cosine, sine_v, kv_own, kv_other],
        [SMEM],
        [pltpu.VMEM((heads * per_chunk, HD), BF16), pltpu.VMEM((2, total, HD), BF16)],
    )

    lines = call(
        stack_kernel,
        [(4, cut, width)] * 2,
        [low]
        + [partner(low, "x", s) for s in (1, 2, 3)]
        + [high]
        + [partner(high, "y", s) for s in (1, 2, 3)],
    )
    gathered = (
        [lines[0]]
        + [partner(lines[0], "y", t) for t in (1, 2, 3)]
        + [lines[1]]
        + [partner(lines[1], "x", t) for t in (1, 2, 3)]
    )
    kept, sent = call(
        output_kernel,
        [(Y * X // 2, per_chunk, features)] * 2,
        [place, *gathered, w_output],
        [SMEM],
        [pltpu.VMEM((Y * X, per_chunk, features), BF16)],
    )
    kept, sent = kept.reshape(half, features), sent.reshape(half, features)
    chip = call(chip_kernel, [(per_row, features)] * 4, [kept, partner(sent, "core", 1)])
    blocks = [chip[0]] + [partner(chip[s], "zl", s) for s in (3, 2, 1)]
    return functools.reduce(jnp.add, [b.astype(F32) for b in blocks]).astype(BF16)


def solution(mesh):
    fine = Mesh(
        mesh.devices.reshape(Z_LO, CORE, Z_HI, Y, X), ("zl", "core", "zh", "y", "x")
    )
    return jax.shard_map(
        shards,
        mesh=fine,
        in_specs=(P(ROW, COL), P(COL, ROW), P(COL, ROW), P(ROW, COL)),
        out_specs=P(ROW, COL),
        check_vma=False,
    )
```

```python
import functools
import math

import jax
import jax.numpy as jnp
from jax import lax
from jax.experimental import pallas as pl
from jax.experimental.pallas import tpu as pltpu
from jax.sharding import Mesh
from jax.sharding import PartitionSpec as P

HD = 128
Z_LO, CORE, Z_HI, Y, X = 4, 2, 2, 4, 4
ROW = ("zl", "core")
COL = ("zh", "y", "x")
PLANE = ("y", "x")
BF16 = jnp.bfloat16
F32 = jnp.float32
VMEM = pl.BlockSpec(memory_space=pltpu.VMEM)
SMEM = pl.BlockSpec(memory_space=pltpu.SMEM)


def tables(positions, width):
    half_width = width // 2
    frequency = 500000.0 ** (-(jnp.arange(half_width).astype(F32) * 2.0 / width))
    angle_v = positions[:, None] * frequency[None, :]
    cosine, sine_v = jnp.cos(angle_v), jnp.sin(angle_v)
    return jnp.concatenate([cosine, cosine], 1), jnp.concatenate([-sine_v, sine_v], 1)


def rotate(values_in, cosine, sine_v):
    return values_in * cosine + pltpu.roll(values_in, HD // 2, 1) * sine_v


def partner(block, axis, step):
    size = {"zl": Z_LO, "core": CORE, "zh": Z_HI, "y": Y, "x": X}[axis]
    return lax.ppermute(block, axis, [(i, i ^ step) for i in range(size)])


def across_plane(block, step, second):
    pairs = []
    for c in range(CORE):
        for y in range(Y):
            for x in range(X):
                along_x = (c == 0) != second
                to_y, to_x = (y, x ^ step) if along_x else (y ^ step, x)
                pairs.append(((c * Y + y) * X + x, (c * Y + to_y) * X + to_x))
    return lax.ppermute(block, ("core", *PLANE), pairs)


def project(block, w_query, w_kv, chunks, k):
    size = chunks.shape[1]
    width = w_query.shape[1]
    query = jnp.dot(block[...], w_query[...], preferred_element_type=F32).astype(BF16)
    keyval = jnp.dot(block[...], w_kv[...], preferred_element_type=F32).astype(BF16)
    for b in range(2):
        part = slice(b * size, (b + 1) * size)
        chunks[k + b, :, :width] = query[part]
        chunks[k + b, :, width:] = keyval[part]


def early_kernel(*refs):
    blocks, w_query, w_kv, out = refs[:2], *refs[2:]
    for i, block in enumerate(blocks):
        project(block, w_query, w_kv, out, 2 * i)


def late_kernel(place, *refs):
    blocks, w_query, w_kv, early = refs[:6], *refs[6:9]
    outs, chunks = refs[9:13], refs[13]
    for side in range(2):
        chunks[8 * side] = early[2 * side]
        chunks[8 * side + 1] = early[2 * side + 1]
        for i in range(3):
            project(blocks[3 * side + i], w_query, w_kv, chunks, 8 * side + 2 * i + 2)
    for s in range(4):
        for j in range(4):
            outs[s][j] = chunks[chunk_at(place, place[0] ^ s, j)]


def chunk_at(place, first, second):
    return first * place[2] + second * place[3]


def halve_kernel(place, a, b, c, d, *outs):
    for t, out in enumerate(outs):
        j = place[1] ^ t
        total = a[j].astype(F32) + b[j].astype(F32) + c[j].astype(F32) + d[j].astype(F32)
        out[...] = total.astype(out.dtype)


def join_kernel(a, b, c, d, query, keyval):
    width = query.shape[1]
    total = a[...] + b[...].astype(F32) + c[...].astype(F32) + d[...].astype(F32)
    query[...] = total[:, :width].astype(BF16)
    keyval[...] = total[:, width:].astype(BF16)


def keys_kernel(a, b, cosine, sine_v, out):
    total = (a[...].astype(F32) + b[...].astype(F32)).astype(BF16).astype(F32)
    block = rotate(total, cosine[...], sine_v[...]).astype(BF16)
    for c in range(out.shape[0]):
        out[c] = block


def attention_kernel(
    heads, base, own, got, cosine, sine_v, kv_own, kv_other, out, queries, pair
):
    per_chunk = own.shape[0]
    pair[0] = kv_own[...]
    for s in range(4):
        part = slice(s * 2 * HD, (s + 1) * 2 * HD)
        pair[1, part, :] = kv_other[(s ^ 1) * 2 * HD : ((s ^ 1) + 1) * 2 * HD, :]
    for h in range(heads):
        cols = slice(h * HD, (h + 1) * HD)
        total = own[:, cols].astype(F32) + got[:, cols].astype(F32)
        queries[h * per_chunk : (h + 1) * per_chunk, :] = rotate(
            total, cosine[...], sine_v[...]
        ).astype(BF16)
    query = queries[...]
    core = base[9]
    rows = heads * per_chunk
    row_pos = base[8] + lax.broadcasted_iota(jnp.int32, (rows, HD), 0) % per_chunk
    lane = lax.broadcasted_iota(jnp.int32, (rows, HD), 1)
    score_scale = 1.0 / math.sqrt(HD)
    totals = jnp.zeros((rows, 1), F32)
    mixed = jnp.zeros((rows, HD), F32)
    for s in range(4):
        part = slice(s * 2 * HD, (s + 1) * 2 * HD)
        keys, values = pair[core, part, :], pair[1 - core, part, :]
        scores = (
            lax.dot_general(query, keys, (((1,), (1,)), ((), ())), preferred_element_type=F32)
            * score_scale
        )
        causal = jnp.concatenate(
            [base[2 * s] + lane <= row_pos, base[2 * s + 1] + lane <= row_pos], 1
        )
        weights = jnp.where(causal, jnp.exp(jnp.where(causal, scores, 0.0)), 0.0)
        totals += jnp.sum(weights, 1, keepdims=True)
        mixed += jnp.dot(weights.astype(BF16), values, preferred_element_type=F32)
    attended = (mixed / totals).astype(BF16)
    for h in range(heads):
        out[:, h * HD : (h + 1) * HD] = attended[h * per_chunk : (h + 1) * per_chunk]


def stack_kernel(*refs):
    for s, ref in enumerate(refs[:4]):
        refs[4][s] = ref[...]


def output_kernel(place, *refs):
    lines, weight, kept, sent, chunks = refs[:4], *refs[4:]
    rows, width = lines[0].shape[1:]
    for t, line in enumerate(lines):
        block = line[...].reshape(4 * rows, width)
        product = jnp.dot(block, weight[...], preferred_element_type=F32).astype(BF16)
        for s in range(4):
            k = chunk_at(place, place[0] ^ s, place[1] ^ t)
            chunks[k] = product[s * rows : (s + 1) * rows]
    half = kept.shape[0]
    kept[...] = chunks[:half]
    sent[...] = chunks[half:]


def chip_kernel(kept, got, *outs):
    rows = outs[0].shape[0]
    for s, out in enumerate(outs):
        part = slice(s * rows, (s + 1) * rows)
        out[...] = (kept[part, :].astype(F32) + got[part, :].astype(F32)).astype(BF16)


def call(kernel, outs, args, specs=(), scratch=()):
    specs = list(specs) + [VMEM] * (len(args) - len(specs))
    return pl.pallas_call(
        kernel,
        out_shape=[
            s if isinstance(s, jax.ShapeDtypeStruct) else jax.ShapeDtypeStruct(s, BF16)
            for s in outs
        ],
        in_specs=specs,
        out_specs=[VMEM] * len(outs),
        scratch_shapes=list(scratch),
        compiler_params=pltpu.CompilerParams(vmem_limit_bytes=32 * 1024 * 1024),
    )(*args)


def shards(tokens, w_query, w_keyval, w_output):
    zl = lax.axis_index("zl")
    core = lax.axis_index("core")
    y = lax.axis_index("y")
    x = lax.axis_index("x")
    per_row, features = tokens.shape
    half = per_row * Z_LO
    total = half * 2
    per_chunk = total // (Y * X)
    width = w_query.shape[1]
    heads = width // HD
    both = width + HD

    mine = [tokens] + [partner(tokens, "zl", s) for s in (1, 2, 3)]

    def block_start(chip, side, index):
        return (((chip ^ (index & 3)) << 1) + ((index >> 2) ^ side)) * per_row

    chunk = y * X + x
    offset = (chunk & 1) * per_chunk
    source_chip, source_core = (zl >> 1) + 2 * core, zl & 1
    row_start = block_start(zl, core, chunk >> 1) + offset
    key_start = block_start(source_chip, source_core, chunk >> 1) + offset
    starts = [block_start(source_chip, source_core, i) for i in range(8)]
    base = jnp.stack([*starts, row_start, core]).astype(jnp.int32)
    steps = jnp.arange(per_chunk)
    cosine, sine_v = tables((row_start + steps).astype(F32), HD)
    key_cos, key_sin = tables((key_start + steps).astype(F32), HD)
    key_cos = jnp.where(core == 0, key_cos, 1.0)
    key_sin = jnp.where(core == 0, key_sin, 0.0)
    first, second = jnp.where(core == 0, x, y), jnp.where(core == 0, y, x)
    place = jnp.stack([first, second, 1 + 3 * core, 4 - 3 * core]).astype(jnp.int32)

    near = partner(tokens, "core", 1)
    (early,) = call(early_kernel, [(4, per_chunk, both)], [tokens, near, w_query, w_keyval])
    *far, early = lax.optimization_barrier((*mine[1:], early))
    parts = call(
        late_kernel,
        [(4, per_chunk, both)] * 4,
        [place, *far, *[partner(block, "core", 1) for block in far], w_query, w_keyval, early],
        [SMEM],
        [pltpu.VMEM((Y * X, per_chunk, both), BF16)],
    )
    got = [across_plane(parts[s], s, False) for s in (1, 2, 3)]
    halves = call(
        halve_kernel,
        [jax.ShapeDtypeStruct((per_chunk, both), F32), *[(per_chunk, both)] * 3],
        [place, parts[0], *got],
        [SMEM],
    )
    got = [across_plane(halves[t], t, True) for t in (1, 2, 3)]
    own, kv = call(join_kernel, [(per_chunk, width), (per_chunk, HD)], [halves[0], *got])
    got = partner(own, "zh", 1)

    moves = [(e, 2 * (e % 4) + e // 4) for e in range(8)]
    here = lax.ppermute(kv, ROW, moves)
    across = lax.ppermute(
        kv, (*ROW, "zh"), [(2 * e + h, 2 * r + 1 - h) for e, r in moves for h in range(2)]
    )
    here, across, got = lax.optimization_barrier((here, across, got))
    (kv_block,) = call(keys_kernel, [(Y * X, per_chunk, HD)], [here, across, key_cos, key_sin])
    kv_own = lax.all_to_all(kv_block, PLANE, 0, 0, tiled=True).reshape(total, HD)
    kv_other = partner(kv_own, "core", 1)
    (attended,) = call(
        functools.partial(attention_kernel, heads),
        [(per_chunk, width)],
        [base, own, got, cosine, sine_v, kv_own, kv_other],
        [SMEM],
        [pltpu.VMEM((heads * per_chunk, HD), BF16), pltpu.VMEM((2, total, HD), BF16)],
    )

    (line,) = call(
        stack_kernel,
        [(4, per_chunk, width)],
        [attended] + [across_plane(attended, s, False) for s in (1, 2, 3)],
    )
    gathered = [line] + [across_plane(line, t, True) for t in (1, 2, 3)]
    kept, sent = call(
        output_kernel,
        [(Y * X // 2, per_chunk, features)] * 2,
        [place, *gathered, w_output],
        [SMEM],
        [pltpu.VMEM((Y * X, per_chunk, features), BF16)],
    )
    kept, sent = kept.reshape(half, features), sent.reshape(half, features)
    chip = call(chip_kernel, [(per_row, features)] * 4, [kept, partner(sent, "core", 1)])
    blocks = [chip[0]] + [partner(chip[s], "zl", s) for s in (3, 2, 1)]
    return functools.reduce(jnp.add, [b.astype(F32) for b in blocks]).astype(BF16)


def solution(mesh):
    fine = Mesh(
        mesh.devices.reshape(Z_LO, CORE, Z_HI, Y, X), ("zl", "core", "zh", "y", "x")
    )
    return jax.shard_map(
        shards,
        mesh=fine,
        in_specs=(P(ROW, COL), P(COL, ROW), P(COL, ROW), P(ROW, COL)),
        out_specs=P(ROW, COL),
        check_vma=False,
    )
```

```python
import functools
import math

import jax
import jax.numpy as jnp
from jax import lax
from jax.experimental import pallas as pl
from jax.experimental.pallas import tpu as pltpu
from jax.sharding import Mesh
from jax.sharding import PartitionSpec as P

HD = 128
Z_LO, CORE, Z_HI, Y, X = 4, 2, 2, 4, 4
ROW = ("zl", "core")
COL = ("zh", "y", "x")
PLANE = ("y", "x")
BF16 = jnp.bfloat16
F32 = jnp.float32
VMEM = pl.BlockSpec(memory_space=pltpu.VMEM)
SMEM = pl.BlockSpec(memory_space=pltpu.SMEM)


def tables(positions, width):
    half_width = width // 2
    frequency = 500000.0 ** (-(jnp.arange(half_width).astype(F32) * 2.0 / width))
    angle_v = positions[:, None] * frequency[None, :]
    cosine, sine_v = jnp.cos(angle_v), jnp.sin(angle_v)
    return jnp.concatenate([cosine, cosine], 1), jnp.concatenate([-sine_v, sine_v], 1)


def rotate(values_in, cosine, sine_v):
    return values_in * cosine + pltpu.roll(values_in, HD // 2, 1) * sine_v


def partner(block, axis, step):
    size = {"zl": Z_LO, "core": CORE, "zh": Z_HI, "y": Y, "x": X}[axis]
    return lax.ppermute(block, axis, [(i, i ^ step) for i in range(size)])


def across_plane(block, step, second):
    pairs = []
    for c in range(CORE):
        for y in range(Y):
            for x in range(X):
                along_x = (c == 0) != second
                to_y, to_x = (y, x ^ step) if along_x else (y ^ step, x)
                pairs.append(((c * Y + y) * X + x, (c * Y + to_y) * X + to_x))
    return lax.ppermute(block, ("core", *PLANE), pairs)


def project(block, w_query, w_kv, chunks, k):
    size = chunks.shape[1]
    width = w_query.shape[1]
    query = jnp.dot(block[...], w_query[...], preferred_element_type=F32).astype(BF16)
    keyval = jnp.dot(block[...], w_kv[...], preferred_element_type=F32).astype(BF16)
    for b in range(2):
        part = slice(b * size, (b + 1) * size)
        chunks[k + b, :, :width] = query[part]
        chunks[k + b, :, width:] = keyval[part]


def early_kernel(*refs):
    blocks, w_query, w_kv, out = refs[:2], *refs[2:]
    for i, block in enumerate(blocks):
        project(block, w_query, w_kv, out, 2 * i)


def late_kernel(place, *refs):
    blocks, w_query, w_kv, early = refs[:6], *refs[6:9]
    outs, chunks = refs[9:13], refs[13]
    for side in range(2):
        chunks[8 * side] = early[2 * side]
        chunks[8 * side + 1] = early[2 * side + 1]
        for i in range(3):
            project(blocks[3 * side + i], w_query, w_kv, chunks, 8 * side + 2 * i + 2)
    for s in range(4):
        for j in range(4):
            outs[s][j] = chunks[(place[0] ^ s) + 4 * j]


def halve_kernel(place, a, b, c, d, *outs):
    for t, out in enumerate(outs):
        j = place[1] ^ t
        total = a[j].astype(F32) + b[j].astype(F32) + c[j].astype(F32) + d[j].astype(F32)
        out[...] = total.astype(out.dtype)


def join_kernel(a, b, c, d, query, keyval):
    width = query.shape[1]
    total = a[...] + b[...].astype(F32) + c[...].astype(F32) + d[...].astype(F32)
    query[...] = total[:, :width].astype(BF16)
    keyval[...] = total[:, width:].astype(BF16)


def keys_kernel(a, b, cosine, sine_v, out):
    total = (a[...].astype(F32) + b[...].astype(F32)).astype(BF16).astype(F32)
    out[...] = rotate(total, cosine[...], sine_v[...]).astype(BF16)


def attention_kernel(heads, base, own, got, cosine, sine_v, *refs):
    kv_own, kv_other, out, queries, pair = refs[:4], refs[4:8], *refs[8:]
    per_chunk = own.shape[0]
    first, second, by_first, by_second = base[10], base[11], base[12], base[13]
    for t in range(4):
        for s in range(4):
            pair[0, by_first * (first ^ s) + by_second * (second ^ t)] = kv_own[t][s]
            k = by_second * (second ^ s) + by_first * (first ^ t)
            pair[1, k ^ 4] = kv_other[t][s]
    for h in range(heads):
        cols = slice(h * HD, (h + 1) * HD)
        total = own[:, cols].astype(F32) + got[:, cols].astype(F32)
        queries[h * per_chunk : (h + 1) * per_chunk, :] = rotate(
            total, cosine[...], sine_v[...]
        ).astype(BF16)
    query = queries[...]
    core = base[9]
    rows = heads * per_chunk
    row_pos = base[8] + lax.broadcasted_iota(jnp.int32, (rows, HD), 0) % per_chunk
    lane = lax.broadcasted_iota(jnp.int32, (rows, HD), 1)
    score_scale = 1.0 / math.sqrt(HD)
    totals = jnp.zeros((rows, 1), F32)
    mixed = jnp.zeros((rows, HD), F32)
    for s in range(4):
        keys = pair[core, 4 * s : 4 * s + 4].reshape(4 * per_chunk, HD)
        values = pair[1 - core, 4 * s : 4 * s + 4].reshape(4 * per_chunk, HD)
        scores = (
            lax.dot_general(query, keys, (((1,), (1,)), ((), ())), preferred_element_type=F32)
            * score_scale
        )
        causal = jnp.concatenate(
            [base[2 * s] + lane <= row_pos, base[2 * s + 1] + lane <= row_pos], 1
        )
        weights = jnp.where(causal, jnp.exp(jnp.where(causal, scores, 0.0)), 0.0)
        totals += jnp.sum(weights, 1, keepdims=True)
        mixed += jnp.dot(weights.astype(BF16), values, preferred_element_type=F32)
    attended = (mixed / totals).astype(BF16)
    for h in range(heads):
        out[:, h * HD : (h + 1) * HD] = attended[h * per_chunk : (h + 1) * per_chunk]


def stack_kernel(*refs):
    for s, ref in enumerate(refs[:4]):
        refs[4][s] = ref[...]


def output_kernel(place, *refs):
    lines, weight, kept, sent, chunks = refs[:4], *refs[4:]
    rows, width = lines[0].shape[1:]
    for t, line in enumerate(lines):
        block = line[...].reshape(4 * rows, width)
        product = jnp.dot(block, weight[...], preferred_element_type=F32).astype(BF16)
        for s in range(4):
            chunks[(place[0] ^ s) + 4 * (place[1] ^ t)] = product[s * rows : (s + 1) * rows]
    half = kept.shape[0]
    kept[...] = chunks[:half]
    sent[...] = chunks[half:]


def chip_kernel(kept, got, *outs):
    rows = outs[0].shape[0]
    for s, out in enumerate(outs):
        part = slice(s * rows, (s + 1) * rows)
        out[...] = (kept[part, :].astype(F32) + got[part, :].astype(F32)).astype(BF16)


def call(kernel, outs, args, specs=(), scratch=()):
    specs = list(specs) + [VMEM] * (len(args) - len(specs))
    return pl.pallas_call(
        kernel,
        out_shape=[
            s if isinstance(s, jax.ShapeDtypeStruct) else jax.ShapeDtypeStruct(s, BF16)
            for s in outs
        ],
        in_specs=specs,
        out_specs=[VMEM] * len(outs),
        scratch_shapes=list(scratch),
        compiler_params=pltpu.CompilerParams(vmem_limit_bytes=32 * 1024 * 1024),
    )(*args)


def shards(tokens, w_query, w_keyval, w_output):
    zl = lax.axis_index("zl")
    core = lax.axis_index("core")
    y = lax.axis_index("y")
    x = lax.axis_index("x")
    per_row, features = tokens.shape
    half = per_row * Z_LO
    total = half * 2
    per_chunk = total // (Y * X)
    width = w_query.shape[1]
    heads = width // HD
    both = width + HD

    mine = [tokens] + [partner(tokens, "zl", s) for s in (1, 2, 3)]

    def block_start(chip, side, index):
        return (((chip ^ (index & 3)) << 1) + ((index >> 2) ^ side)) * per_row

    first, second = jnp.where(core == 0, x, y), jnp.where(core == 0, y, x)
    source_chip, source_core = (zl >> 1) + 2 * core, zl & 1
    by_first = jnp.where(source_core == core, 1, 4)
    by_second = 5 - by_first
    chunk = first + 4 * second
    key_chunk = by_first * first + by_second * second
    row_start = block_start(zl, core, chunk >> 1) + (chunk & 1) * per_chunk
    key_start = block_start(source_chip, source_core, key_chunk >> 1) + (key_chunk & 1) * per_chunk
    starts = [block_start(source_chip, source_core, i) for i in range(8)]
    base = jnp.stack([*starts, row_start, core, first, second, by_first, by_second]).astype(
        jnp.int32
    )
    steps = jnp.arange(per_chunk)
    cosine, sine_v = tables((row_start + steps).astype(F32), HD)
    key_cos, key_sin = tables((key_start + steps).astype(F32), HD)
    key_cos = jnp.where(core == 0, key_cos, 1.0)
    key_sin = jnp.where(core == 0, key_sin, 0.0)
    place = jnp.stack([first, second]).astype(jnp.int32)

    near = partner(tokens, "core", 1)
    (early,) = call(early_kernel, [(4, per_chunk, both)], [tokens, near, w_query, w_keyval])
    *far, early = lax.optimization_barrier((*mine[1:], early))
    parts = call(
        late_kernel,
        [(4, per_chunk, both)] * 4,
        [place, *far, *[partner(block, "core", 1) for block in far], w_query, w_keyval, early],
        [SMEM],
        [pltpu.VMEM((Y * X, per_chunk, both), BF16)],
    )
    got = [across_plane(parts[s], s, False) for s in (1, 2, 3)]
    halves = call(
        halve_kernel,
        [jax.ShapeDtypeStruct((per_chunk, both), F32), *[(per_chunk, both)] * 3],
        [place, parts[0], *got],
        [SMEM],
    )
    got = [across_plane(halves[t], t, True) for t in (1, 2, 3)]
    own, kv = call(join_kernel, [(per_chunk, width), (per_chunk, HD)], [halves[0], *got])
    moves = [(e, 2 * (e % 4) + e // 4) for e in range(8)]
    here = lax.ppermute(kv, ROW, moves)
    across = lax.ppermute(
        kv, (*ROW, "zh"), [(2 * e + h, 2 * r + 1 - h) for e, r in moves for h in range(2)]
    )
    got = partner(own, "zh", 1)
    (kv_block,) = call(keys_kernel, [(per_chunk, HD)], [here, across, key_cos, key_sin])
    (kv_line,) = call(
        stack_kernel,
        [(4, per_chunk, HD)],
        [kv_block] + [across_plane(kv_block, s, False) for s in (1, 2, 3)],
    )
    kv_own = [kv_line] + [across_plane(kv_line, t, True) for t in (1, 2, 3)]
    kv_other = [partner(lines, "core", 1) for lines in kv_own]
    (attended,) = call(
        functools.partial(attention_kernel, heads),
        [(per_chunk, width)],
        [base, own, got, cosine, sine_v, *kv_own, *kv_other],
        [SMEM],
        [
            pltpu.VMEM((heads * per_chunk, HD), BF16),
            pltpu.VMEM((2, Y * X, per_chunk, HD), BF16),
        ],
    )

    (line,) = call(
        stack_kernel,
        [(4, per_chunk, width)],
        [attended] + [across_plane(attended, s, False) for s in (1, 2, 3)],
    )
    gathered = [line] + [across_plane(line, t, True) for t in (1, 2, 3)]
    kept, sent = call(
        output_kernel,
        [(Y * X // 2, per_chunk, features)] * 2,
        [place, *gathered, w_output],
        [SMEM],
        [pltpu.VMEM((Y * X, per_chunk, features), BF16)],
    )
    kept, sent = kept.reshape(half, features), sent.reshape(half, features)
    chip = call(chip_kernel, [(per_row, features)] * 4, [kept, partner(sent, "core", 1)])
    blocks = [chip[0]] + [partner(chip[s], "zl", s) for s in (3, 2, 1)]
    return functools.reduce(jnp.add, [b.astype(F32) for b in blocks]).astype(BF16)


def solution(mesh):
    fine = Mesh(
        mesh.devices.reshape(Z_LO, CORE, Z_HI, Y, X), ("zl", "core", "zh", "y", "x")
    )
    return jax.shard_map(
        shards,
        mesh=fine,
        in_specs=(P(ROW, COL), P(COL, ROW), P(COL, ROW), P(ROW, COL)),
        out_specs=P(ROW, COL),
        check_vma=False,
    )
```

```python
import functools
import math

import jax
import jax.numpy as jnp
from jax import lax
from jax.experimental import pallas as pl
from jax.experimental.pallas import tpu as pltpu
from jax.sharding import Mesh
from jax.sharding import PartitionSpec as P

HD = 128
Z_LO, CORE, Z_HI, Y, X = 4, 2, 2, 4, 4
ROW = ("zl", "core")
COL = ("zh", "y", "x")
PLANE = ("y", "x")
BF16 = jnp.bfloat16
F32 = jnp.float32
VMEM = pl.BlockSpec(memory_space=pltpu.VMEM)
SMEM = pl.BlockSpec(memory_space=pltpu.SMEM)


def tables(positions, width):
    half_width = width // 2
    frequency = 500000.0 ** (-(jnp.arange(half_width).astype(F32) * 2.0 / width))
    angle_v = positions[:, None] * frequency[None, :]
    cosine, sine_v = jnp.cos(angle_v), jnp.sin(angle_v)
    return jnp.concatenate([cosine, cosine], 1), jnp.concatenate([-sine_v, sine_v], 1)


def rotate(values_in, cosine, sine_v):
    return values_in * cosine + pltpu.roll(values_in, HD // 2, 1) * sine_v


def partner(block, axis, step):
    size = {"zl": Z_LO, "core": CORE, "zh": Z_HI, "y": Y, "x": X}[axis]
    return lax.ppermute(block, axis, [(i, i ^ step) for i in range(size)])


def across_plane(block, step, second):
    pairs = []
    for c in range(CORE):
        for y in range(Y):
            for x in range(X):
                along_x = (c == 0) != second
                to_y, to_x = (y, x ^ step) if along_x else (y ^ step, x)
                pairs.append(((c * Y + y) * X + x, (c * Y + to_y) * X + to_x))
    return lax.ppermute(block, ("core", *PLANE), pairs)


def project(block, w_query, w_kv, chunks, k):
    size = chunks.shape[1]
    width = w_query.shape[1]
    query = jnp.dot(block[...], w_query[...], preferred_element_type=F32).astype(BF16)
    keyval = jnp.dot(block[...], w_kv[...], preferred_element_type=F32).astype(BF16)
    for b in range(2):
        part = slice(b * size, (b + 1) * size)
        chunks[k + b, :, :width] = query[part]
        chunks[k + b, :, width:] = keyval[part]


def early_kernel(*refs):
    blocks, w_query, w_kv, out = refs[:2], *refs[2:]
    for i, block in enumerate(blocks):
        project(block, w_query, w_kv, out, 2 * i)


def late_kernel(place, *refs):
    blocks, w_query, w_kv, early = refs[:6], *refs[6:9]
    outs, late = refs[9:13], refs[13]
    in_y = place[2] == 4

    def put(k, source, row):
        first = jnp.where(in_y, k >> 2, k & 3)
        second = jnp.where(in_y, k & 3, k >> 2)
        for s, out in enumerate(outs):

            @pl.when((first ^ place[0]) == s)
            def _():
                out[second] = source[row]

    for side in range(2):
        for b in range(2):
            put(8 * side + b, early, 2 * side + b)
        for i in range(3):
            row = 6 * side + 2 * i
            project(blocks[3 * side + i], w_query, w_kv, late, row)
            for b in range(2):
                put(8 * side + 2 * i + 2 + b, late, row + b)


def chunk_at(place, first, second):
    return first * place[2] + second * place[3]


def halve_kernel(place, a, b, c, d, *outs):
    for t, out in enumerate(outs):
        j = place[1] ^ t
        total = a[j].astype(F32) + b[j].astype(F32) + c[j].astype(F32) + d[j].astype(F32)
        out[...] = total.astype(out.dtype)


def join_kernel(a, b, c, d, query, keyval):
    width = query.shape[1]
    total = a[...] + b[...].astype(F32) + c[...].astype(F32) + d[...].astype(F32)
    query[...] = total[:, :width].astype(BF16)
    keyval[...] = total[:, width:].astype(BF16)


def keys_kernel(a, b, cosine, sine_v, out):
    total = (a[...].astype(F32) + b[...].astype(F32)).astype(BF16).astype(F32)
    block = rotate(total, cosine[...], sine_v[...]).astype(BF16)
    for c in range(out.shape[0]):
        out[c] = block


def attention_kernel(
    heads, base, own, got, cosine, sine_v, kv_own, kv_other, out, queries, pair
):
    per_chunk = own.shape[0]
    pair[0] = kv_own[...]
    for s in range(4):
        part = slice(s * 2 * HD, (s + 1) * 2 * HD)
        pair[1, part, :] = kv_other[(s ^ 1) * 2 * HD : ((s ^ 1) + 1) * 2 * HD, :]
    for h in range(heads):
        cols = slice(h * HD, (h + 1) * HD)
        total = own[:, cols].astype(F32) + got[:, cols].astype(F32)
        queries[h * per_chunk : (h + 1) * per_chunk, :] = rotate(
            total, cosine[...], sine_v[...]
        ).astype(BF16)
    query = queries[...]
    core = base[9]
    rows = heads * per_chunk
    row_pos = base[8] + lax.broadcasted_iota(jnp.int32, (rows, HD), 0) % per_chunk
    lane = lax.broadcasted_iota(jnp.int32, (rows, HD), 1)
    score_scale = 1.0 / math.sqrt(HD)
    totals = jnp.zeros((rows, 1), F32)
    mixed = jnp.zeros((rows, HD), F32)
    for s in range(4):
        part = slice(s * 2 * HD, (s + 1) * 2 * HD)
        keys, values = pair[core, part, :], pair[1 - core, part, :]
        scores = (
            lax.dot_general(query, keys, (((1,), (1,)), ((), ())), preferred_element_type=F32)
            * score_scale
        )
        causal = jnp.concatenate(
            [base[2 * s] + lane <= row_pos, base[2 * s + 1] + lane <= row_pos], 1
        )
        weights = jnp.where(causal, jnp.exp(jnp.where(causal, scores, 0.0)), 0.0)
        totals += jnp.sum(weights, 1, keepdims=True)
        mixed += jnp.dot(weights.astype(BF16), values, preferred_element_type=F32)
    attended = (mixed / totals).astype(BF16)
    for h in range(heads):
        out[:, h * HD : (h + 1) * HD] = attended[h * per_chunk : (h + 1) * per_chunk]


def stack_kernel(*refs):
    for s, ref in enumerate(refs[:4]):
        refs[4][s] = ref[...]


def line_kernel(line, weight, out):
    rows, width = line.shape[1:]
    block = line[...].reshape(4 * rows, width)
    product = jnp.dot(block, weight[...], preferred_element_type=F32).astype(BF16)
    for s in range(4):
        out[s] = product[s * rows : (s + 1) * rows]


def output_kernel(place, *refs):
    early, line, weight, kept, sent, last, chunks = refs[:3], *refs[3:]
    line_kernel(line, weight, last)
    for t, part in enumerate([*early, last]):
        for s in range(4):
            chunks[chunk_at(place, place[0] ^ s, place[1] ^ t)] = part[s]
    half = kept.shape[0]
    kept[...] = chunks[:half]
    sent[...] = chunks[half:]


def chip_kernel(kept, got, *outs):
    rows = outs[0].shape[0]
    for s, out in enumerate(outs):
        part = slice(s * rows, (s + 1) * rows)
        out[...] = (kept[part, :].astype(F32) + got[part, :].astype(F32)).astype(BF16)


def call(kernel, outs, args, specs=(), scratch=()):
    specs = list(specs) + [VMEM] * (len(args) - len(specs))
    return pl.pallas_call(
        kernel,
        out_shape=[
            s if isinstance(s, jax.ShapeDtypeStruct) else jax.ShapeDtypeStruct(s, BF16)
            for s in outs
        ],
        in_specs=specs,
        out_specs=[VMEM] * len(outs),
        scratch_shapes=list(scratch),
        compiler_params=pltpu.CompilerParams(vmem_limit_bytes=32 * 1024 * 1024),
    )(*args)


def shards(tokens, w_query, w_keyval, w_output):
    zl = lax.axis_index("zl")
    core = lax.axis_index("core")
    y = lax.axis_index("y")
    x = lax.axis_index("x")
    per_row, features = tokens.shape
    half = per_row * Z_LO
    total = half * 2
    per_chunk = total // (Y * X)
    width = w_query.shape[1]
    heads = width // HD
    both = width + HD

    mine = [tokens] + [partner(tokens, "zl", s) for s in (1, 2, 3)]

    def block_start(chip, side, index):
        return (((chip ^ (index & 3)) << 1) + ((index >> 2) ^ side)) * per_row

    chunk = y * X + x
    offset = (chunk & 1) * per_chunk
    source_chip, source_core = (zl >> 1) + 2 * core, zl & 1
    row_start = block_start(zl, core, chunk >> 1) + offset
    key_start = block_start(source_chip, source_core, chunk >> 1) + offset
    starts = [block_start(source_chip, source_core, i) for i in range(8)]
    base = jnp.stack([*starts, row_start, core]).astype(jnp.int32)
    steps = jnp.arange(per_chunk)
    cosine, sine_v = tables((row_start + steps).astype(F32), HD)
    key_cos, key_sin = tables((key_start + steps).astype(F32), HD)
    key_cos = jnp.where(core == 0, key_cos, 1.0)
    key_sin = jnp.where(core == 0, key_sin, 0.0)
    first, second = jnp.where(core == 0, x, y), jnp.where(core == 0, y, x)
    place = jnp.stack([first, second, 1 + 3 * core, 4 - 3 * core]).astype(jnp.int32)

    near = partner(tokens, "core", 1)
    (early,) = call(early_kernel, [(4, per_chunk, both)], [tokens, near, w_query, w_keyval])
    *far, early = lax.optimization_barrier((*mine[1:], early))
    parts = call(
        late_kernel,
        [(4, per_chunk, both)] * 4,
        [place, *far, *[partner(block, "core", 1) for block in far], w_query, w_keyval, early],
        [SMEM],
        [pltpu.VMEM((12, per_chunk, both), BF16)],
    )
    got = [across_plane(parts[s], s, False) for s in (1, 2, 3)]
    halves = call(
        halve_kernel,
        [jax.ShapeDtypeStruct((per_chunk, both), F32), *[(per_chunk, both)] * 3],
        [place, parts[0], *got],
        [SMEM],
    )
    got = [across_plane(halves[t], t, True) for t in (1, 2, 3)]
    own, kv = call(join_kernel, [(per_chunk, width), (per_chunk, HD)], [halves[0], *got])
    got = partner(own, "zh", 1)

    moves = [(e, 2 * (e % 4) + e // 4) for e in range(8)]
    here = lax.ppermute(kv, ROW, moves)
    across = lax.ppermute(
        kv, (*ROW, "zh"), [(2 * e + h, 2 * r + 1 - h) for e, r in moves for h in range(2)]
    )
    here, across, got = lax.optimization_barrier((here, across, got))
    (kv_block,) = call(keys_kernel, [(Y * X, per_chunk, HD)], [here, across, key_cos, key_sin])
    kv_own = lax.all_to_all(kv_block, PLANE, 0, 0, tiled=True).reshape(total, HD)
    kv_other = partner(kv_own, "core", 1)
    (attended,) = call(
        functools.partial(attention_kernel, heads),
        [(per_chunk, width)],
        [base, own, got, cosine, sine_v, kv_own, kv_other],
        [SMEM],
        [pltpu.VMEM((heads * per_chunk, HD), BF16), pltpu.VMEM((2, total, HD), BF16)],
    )

    (line,) = call(
        stack_kernel,
        [(4, per_chunk, width)],
        [attended] + [across_plane(attended, s, False) for s in (1, 2, 3)],
    )
    gathered = [across_plane(line, t, True) for t in (1, 2, 3)]
    early = []
    for t in range(3):
        (done,) = call(line_kernel, [(4, per_chunk, features)], [line, w_output])
        line, done = lax.optimization_barrier((gathered[t], done))
        early.append(done)
    kept, sent = call(
        output_kernel,
        [(Y * X // 2, per_chunk, features)] * 2,
        [place, *early, line, w_output],
        [SMEM],
        [
            pltpu.VMEM((4, per_chunk, features), BF16),
            pltpu.VMEM((Y * X, per_chunk, features), BF16),
        ],
    )
    kept, sent = kept.reshape(half, features), sent.reshape(half, features)
    chip = call(chip_kernel, [(per_row, features)] * 4, [kept, partner(sent, "core", 1)])
    blocks = [chip[0]] + [partner(chip[s], "zl", s) for s in (3, 2, 1)]
    return functools.reduce(jnp.add, [b.astype(F32) for b in blocks]).astype(BF16)


def solution(mesh):
    fine = Mesh(
        mesh.devices.reshape(Z_LO, CORE, Z_HI, Y, X), ("zl", "core", "zh", "y", "x")
    )
    return jax.shard_map(
        shards,
        mesh=fine,
        in_specs=(P(ROW, COL), P(COL, ROW), P(COL, ROW), P(ROW, COL)),
        out_specs=P(ROW, COL),
        check_vma=False,
    )
```

```python
import functools
import math

import jax
import jax.numpy as jnp
from jax import lax
from jax.experimental import pallas as pl
from jax.experimental.pallas import tpu as pltpu
from jax.sharding import Mesh
from jax.sharding import PartitionSpec as P

HD = 128
Z_LO, CORE, Z_HI, Y, X = 4, 2, 2, 4, 4
ROW = ("zl", "core")
COL = ("zh", "y", "x")
PLANE = ("y", "x")
STEPS = (0, 1, 3, 2)
FAR = (2, 3, 1)
BF16 = jnp.bfloat16
F32 = jnp.float32
VMEM = pl.BlockSpec(memory_space=pltpu.VMEM)
SMEM = pl.BlockSpec(memory_space=pltpu.SMEM)


def tables(positions, width):
    half_width = width // 2
    frequency = 500000.0 ** (-(jnp.arange(half_width).astype(F32) * 2.0 / width))
    angle_v = positions[:, None] * frequency[None, :]
    cosine, sine_v = jnp.cos(angle_v), jnp.sin(angle_v)
    return jnp.concatenate([cosine, cosine], 1), jnp.concatenate([-sine_v, sine_v], 1)


def rotate(values_in, cosine, sine_v):
    return values_in * cosine + pltpu.roll(values_in, HD // 2, 1) * sine_v


def partner(block, axis, step):
    size = {"zl": Z_LO, "core": CORE, "zh": Z_HI, "y": Y, "x": X}[axis]
    return lax.ppermute(block, axis, [(i, i ^ step) for i in range(size)])


def across_plane(block, step, second):
    pairs = []
    for c in range(CORE):
        for y in range(Y):
            for x in range(X):
                along_x = (c == 0) != second
                to_y, to_x = (y, x ^ step) if along_x else (y ^ step, x)
                pairs.append(((c * Y + y) * X + x, (c * Y + to_y) * X + to_x))
    return lax.ppermute(block, ("core", *PLANE), pairs)


def project(block, w_query, w_kv, chunks, k):
    size = chunks.shape[1]
    width = w_query.shape[1]
    query = jnp.dot(block[...], w_query[...], preferred_element_type=F32).astype(BF16)
    keyval = jnp.dot(block[...], w_kv[...], preferred_element_type=F32).astype(BF16)
    for b in range(2):
        part = slice(b * size, (b + 1) * size)
        chunks[k + b, :, :width] = query[part]
        chunks[k + b, :, width:] = keyval[part]


def early_kernel(*refs):
    blocks, w_query, w_kv, out = refs[:2], *refs[2:]
    for i, block in enumerate(blocks):
        project(block, w_query, w_kv, out, 2 * i)


def late_kernel(place, *refs):
    blocks, w_query, w_kv, early = refs[:6], *refs[6:9]
    outs, chunks = refs[9:13], refs[13]
    for side in range(2):
        chunks[8 * side] = early[2 * side]
        chunks[8 * side + 1] = early[2 * side + 1]
        for i in range(3):
            project(blocks[3 * side + i], w_query, w_kv, chunks, 8 * side + 2 * FAR[i])
    for s in range(4):
        for j in range(4):
            outs[s][j] = chunks[chunk_at(place, place[0] ^ s, j)]


def chunk_at(place, first, second):
    return first * place[2] + second * place[3]


def halve_kernel(place, a, b, c, d, *outs):
    for t, out in enumerate(outs):
        j = place[1] ^ t
        total = a[j].astype(F32) + b[j].astype(F32) + c[j].astype(F32) + d[j].astype(F32)
        out[...] = total.astype(out.dtype)


def join_kernel(a, b, c, d, query, keyval):
    width = query.shape[1]
    total = a[...] + b[...].astype(F32) + c[...].astype(F32) + d[...].astype(F32)
    query[...] = total[:, :width].astype(BF16)
    keyval[...] = total[:, width:].astype(BF16)


def keys_kernel(a, b, cosine, sine_v, out):
    total = (a[...].astype(F32) + b[...].astype(F32)).astype(BF16).astype(F32)
    block = rotate(total, cosine[...], sine_v[...]).astype(BF16)
    for c in range(out.shape[0]):
        out[c] = block


def attention_kernel(
    heads, base, own, got, cosine, sine_v, kv_own, kv_other, out, queries, pair
):
    per_chunk = own.shape[0]
    pair[0] = kv_own[...]
    for s in range(4):
        part = slice(s * 2 * HD, (s + 1) * 2 * HD)
        pair[1, part, :] = kv_other[(s ^ 1) * 2 * HD : ((s ^ 1) + 1) * 2 * HD, :]
    for h in range(heads):
        cols = slice(h * HD, (h + 1) * HD)
        total = own[:, cols].astype(F32) + got[:, cols].astype(F32)
        queries[h * per_chunk : (h + 1) * per_chunk, :] = rotate(
            total, cosine[...], sine_v[...]
        ).astype(BF16)
    query = queries[...]
    core = base[9]
    rows = heads * per_chunk
    row_pos = base[8] + lax.broadcasted_iota(jnp.int32, (rows, HD), 0) % per_chunk
    lane = lax.broadcasted_iota(jnp.int32, (rows, HD), 1)
    score_scale = 1.0 / math.sqrt(HD)
    totals = jnp.zeros((rows, 1), F32)
    mixed = jnp.zeros((rows, HD), F32)
    for s in range(4):
        part = slice(s * 2 * HD, (s + 1) * 2 * HD)
        keys, values = pair[core, part, :], pair[1 - core, part, :]
        scores = (
            lax.dot_general(query, keys, (((1,), (1,)), ((), ())), preferred_element_type=F32)
            * score_scale
        )
        causal = jnp.concatenate(
            [base[2 * s] + lane <= row_pos, base[2 * s + 1] + lane <= row_pos], 1
        )
        weights = jnp.where(causal, jnp.exp(jnp.where(causal, scores, 0.0)), 0.0)
        totals += jnp.sum(weights, 1, keepdims=True)
        mixed += jnp.dot(weights.astype(BF16), values, preferred_element_type=F32)
    attended = (mixed / totals).astype(BF16)
    for h in range(heads):
        out[:, h * HD : (h + 1) * HD] = attended[h * per_chunk : (h + 1) * per_chunk]


def stack_kernel(*refs):
    for s, ref in zip(STEPS, refs[:4]):
        refs[4][s] = ref[...]


def line_kernel(line, weight, out):
    rows, width = line.shape[1:]
    block = line[...].reshape(4 * rows, width)
    product = jnp.dot(block, weight[...], preferred_element_type=F32).astype(BF16)
    for s in range(4):
        out[s] = product[s * rows : (s + 1) * rows]


def output_kernel(place, *refs):
    early, line, weight, kept, sent, last, chunks = refs[:3], *refs[3:]
    line_kernel(line, weight, last)
    for t, part in zip(STEPS, [*early, last]):
        for s in range(4):
            chunks[chunk_at(place, place[0] ^ s, place[1] ^ t)] = part[s]
    half = kept.shape[0]
    kept[...] = chunks[:half]
    sent[...] = chunks[half:]


def chip_kernel(kept, got, *outs):
    rows = outs[0].shape[0]
    for s, out in enumerate(outs):
        part = slice(s * rows, (s + 1) * rows)
        out[...] = (kept[part, :].astype(F32) + got[part, :].astype(F32)).astype(BF16)


def call(kernel, outs, args, specs=(), scratch=()):
    specs = list(specs) + [VMEM] * (len(args) - len(specs))
    return pl.pallas_call(
        kernel,
        out_shape=[
            s if isinstance(s, jax.ShapeDtypeStruct) else jax.ShapeDtypeStruct(s, BF16)
            for s in outs
        ],
        in_specs=specs,
        out_specs=[VMEM] * len(outs),
        scratch_shapes=list(scratch),
        compiler_params=pltpu.CompilerParams(vmem_limit_bytes=32 * 1024 * 1024),
    )(*args)


def shards(tokens, w_query, w_keyval, w_output):
    zl = lax.axis_index("zl")
    core = lax.axis_index("core")
    y = lax.axis_index("y")
    x = lax.axis_index("x")
    per_row, features = tokens.shape
    half = per_row * Z_LO
    total = half * 2
    per_chunk = total // (Y * X)
    width = w_query.shape[1]
    heads = width // HD
    both = width + HD

    far = [partner(tokens, "zl", s) for s in FAR]

    def block_start(chip, side, index):
        return (((chip ^ (index & 3)) << 1) + ((index >> 2) ^ side)) * per_row

    chunk = y * X + x
    offset = (chunk & 1) * per_chunk
    source_chip, source_core = (zl >> 1) + 2 * core, zl & 1
    row_start = block_start(zl, core, chunk >> 1) + offset
    key_start = block_start(source_chip, source_core, chunk >> 1) + offset
    starts = [block_start(source_chip, source_core, i) for i in range(8)]
    base = jnp.stack([*starts, row_start, core]).astype(jnp.int32)
    steps = jnp.arange(per_chunk)
    cosine, sine_v = tables((row_start + steps).astype(F32), HD)
    key_cos, key_sin = tables((key_start + steps).astype(F32), HD)
    key_cos = jnp.where(core == 0, key_cos, 1.0)
    key_sin = jnp.where(core == 0, key_sin, 0.0)
    first, second = jnp.where(core == 0, x, y), jnp.where(core == 0, y, x)
    place = jnp.stack([first, second, 1 + 3 * core, 4 - 3 * core]).astype(jnp.int32)

    near = partner(tokens, "core", 1)
    (early,) = call(early_kernel, [(4, per_chunk, both)], [tokens, near, w_query, w_keyval])
    *far, early = lax.optimization_barrier((*far, early))
    parts = call(
        late_kernel,
        [(4, per_chunk, both)] * 4,
        [place, *far, *[partner(block, "core", 1) for block in far], w_query, w_keyval, early],
        [SMEM],
        [pltpu.VMEM((Y * X, per_chunk, both), BF16)],
    )
    got = [across_plane(parts[s], s, False) for s in STEPS[1:]]
    halves = call(
        halve_kernel,
        [jax.ShapeDtypeStruct((per_chunk, both), F32), *[(per_chunk, both)] * 3],
        [place, parts[0], *got],
        [SMEM],
    )
    got = [across_plane(halves[t], t, True) for t in STEPS[1:]]
    own, kv = call(join_kernel, [(per_chunk, width), (per_chunk, HD)], [halves[0], *got])
    got = partner(own, "zh", 1)

    moves = [(e, 2 * (e % 4) + e // 4) for e in range(8)]
    here = lax.ppermute(kv, ROW, moves)
    across = lax.ppermute(
        kv, (*ROW, "zh"), [(2 * e + h, 2 * r + 1 - h) for e, r in moves for h in range(2)]
    )
    here, across, got = lax.optimization_barrier((here, across, got))
    (kv_block,) = call(keys_kernel, [(Y * X, per_chunk, HD)], [here, across, key_cos, key_sin])
    kv_own = lax.all_to_all(kv_block, PLANE, 0, 0, tiled=True).reshape(total, HD)
    kv_other = partner(kv_own, "core", 1)
    (attended,) = call(
        functools.partial(attention_kernel, heads),
        [(per_chunk, width)],
        [base, own, got, cosine, sine_v, kv_own, kv_other],
        [SMEM],
        [pltpu.VMEM((heads * per_chunk, HD), BF16), pltpu.VMEM((2, total, HD), BF16)],
    )

    (line,) = call(
        stack_kernel,
        [(4, per_chunk, width)],
        [attended] + [across_plane(attended, s, False) for s in STEPS[1:]],
    )
    gathered = [across_plane(line, t, True) for t in STEPS[1:]]
    early = []
    for block in gathered:
        (done,) = call(line_kernel, [(4, per_chunk, features)], [line, w_output])
        line, done = lax.optimization_barrier((block, done))
        early.append(done)
    kept, sent = call(
        output_kernel,
        [(Y * X // 2, per_chunk, features)] * 2,
        [place, *early, line, w_output],
        [SMEM],
        [
            pltpu.VMEM((4, per_chunk, features), BF16),
            pltpu.VMEM((Y * X, per_chunk, features), BF16),
        ],
    )
    kept, sent = kept.reshape(half, features), sent.reshape(half, features)
    chip = call(chip_kernel, [(per_row, features)] * 4, [kept, partner(sent, "core", 1)])
    blocks = [chip[0]] + [partner(chip[s], "zl", s) for s in (3, 2, 1)]
    return functools.reduce(jnp.add, [b.astype(F32) for b in blocks]).astype(BF16)


def solution(mesh):
    fine = Mesh(
        mesh.devices.reshape(Z_LO, CORE, Z_HI, Y, X), ("zl", "core", "zh", "y", "x")
    )
    return jax.shard_map(
        shards,
        mesh=fine,
        in_specs=(P(ROW, COL), P(COL, ROW), P(COL, ROW), P(ROW, COL)),
        out_specs=P(ROW, COL),
        check_vma=False,
    )
```

```python
import functools
import math

import jax
import jax.numpy as jnp
from jax import lax
from jax.experimental import pallas as pl
from jax.experimental.pallas import tpu as pltpu
from jax.sharding import Mesh
from jax.sharding import PartitionSpec as P

HD = 128
Z_LO, CORE, Z_HI, Y, X = 4, 2, 2, 4, 4
ROW = ("zl", "core")
COL = ("zh", "y", "x")
PLANE = ("y", "x")
STEPS = (0, 1, 3, 2)
FAR = (2, 3, 1)
BF16 = jnp.bfloat16
F32 = jnp.float32
VMEM = pl.BlockSpec(memory_space=pltpu.VMEM)
SMEM = pl.BlockSpec(memory_space=pltpu.SMEM)


def tables(positions, width):
    half_width = width // 2
    frequency = 500000.0 ** (-(jnp.arange(half_width).astype(F32) * 2.0 / width))
    angle_v = positions[:, None] * frequency[None, :]
    cosine, sine_v = jnp.cos(angle_v), jnp.sin(angle_v)
    return jnp.concatenate([cosine, cosine], 1), jnp.concatenate([-sine_v, sine_v], 1)


def rotate(values_in, cosine, sine_v):
    return values_in * cosine + pltpu.roll(values_in, HD // 2, 1) * sine_v


def partner(block, axis, step):
    size = {"zl": Z_LO, "core": CORE, "zh": Z_HI, "y": Y, "x": X}[axis]
    return lax.ppermute(block, axis, [(i, i ^ step) for i in range(size)])


def across_plane(block, step, second):
    pairs = []
    for c in range(CORE):
        for y in range(Y):
            for x in range(X):
                along_x = (c == 0) != second
                to_y, to_x = (y, x ^ step) if along_x else (y ^ step, x)
                pairs.append(((c * Y + y) * X + x, (c * Y + to_y) * X + to_x))
    return lax.ppermute(block, ("core", *PLANE), pairs)


def project(block, w_query, w_kv, chunks, keyvals, k):
    size = chunks.shape[1]
    query = jnp.dot(block[...], w_query[...], preferred_element_type=F32).astype(BF16)
    keyval = jnp.dot(block[...], w_kv[...], preferred_element_type=F32).astype(BF16)
    for b in range(2):
        part = slice(b * size, (b + 1) * size)
        chunks[k + b] = query[part]
        keyvals[k + b] = keyval[part]


def early_kernel(*refs):
    blocks, w_query, w_kv, out, keyvals = refs[:2], *refs[2:]
    for i, block in enumerate(blocks):
        project(block, w_query, w_kv, out, keyvals, 2 * i)


def late_kernel(place, *refs):
    blocks, w_query, w_kv, early, early_kv = refs[:6], *refs[6:10]
    outs, keyvals, chunks = refs[10:14], refs[14], refs[15]
    for side in range(2):
        for b in range(2):
            chunks[8 * side + b] = early[2 * side + b]
            keyvals[8 * side + b] = early_kv[2 * side + b]
        for i in range(3):
            project(
                blocks[3 * side + i], w_query, w_kv, chunks, keyvals, 8 * side + 2 * FAR[i]
            )
    for s in range(4):
        for j in range(4):
            outs[s][j] = chunks[chunk_at(place, place[0] ^ s, j)]


def chunk_at(place, first, second):
    return first * place[2] + second * place[3]


def halve_kernel(place, a, b, c, d, *outs):
    for t, out in enumerate(outs):
        j = place[1] ^ t
        total = a[j].astype(F32) + b[j].astype(F32) + c[j].astype(F32) + d[j].astype(F32)
        out[...] = total.astype(out.dtype)


def join_kernel(a, b, c, d, out):
    total = a[...] + b[...].astype(F32) + c[...].astype(F32) + d[...].astype(F32)
    out[...] = total.astype(BF16)


def sum_kernel(parts, out):
    total = parts[0].astype(F32)
    for c in range(1, parts.shape[0]):
        total += parts[c].astype(F32)
    out[...] = total.astype(BF16)


def keys_kernel(a, b, cosine, sine_v, out):
    total = (a[...].astype(F32) + b[...].astype(F32)).astype(BF16).astype(F32)
    block = rotate(total, cosine[...], sine_v[...]).astype(BF16)
    for c in range(out.shape[0]):
        out[c] = block


def attention_kernel(
    heads, base, own, got, cosine, sine_v, kv_own, kv_other, out, queries, pair
):
    per_chunk = own.shape[0]
    pair[0] = kv_own[...]
    for s in range(4):
        part = slice(s * 2 * HD, (s + 1) * 2 * HD)
        pair[1, part, :] = kv_other[(s ^ 1) * 2 * HD : ((s ^ 1) + 1) * 2 * HD, :]
    for h in range(heads):
        cols = slice(h * HD, (h + 1) * HD)
        total = own[:, cols].astype(F32) + got[:, cols].astype(F32)
        queries[h * per_chunk : (h + 1) * per_chunk, :] = rotate(
            total, cosine[...], sine_v[...]
        ).astype(BF16)
    query = queries[...]
    core = base[9]
    rows = heads * per_chunk
    row_pos = base[8] + lax.broadcasted_iota(jnp.int32, (rows, HD), 0) % per_chunk
    lane = lax.broadcasted_iota(jnp.int32, (rows, HD), 1)
    score_scale = 1.0 / math.sqrt(HD)
    totals = jnp.zeros((rows, 1), F32)
    mixed = jnp.zeros((rows, HD), F32)
    for s in range(4):
        part = slice(s * 2 * HD, (s + 1) * 2 * HD)
        keys, values = pair[core, part, :], pair[1 - core, part, :]
        scores = (
            lax.dot_general(query, keys, (((1,), (1,)), ((), ())), preferred_element_type=F32)
            * score_scale
        )
        causal = jnp.concatenate(
            [base[2 * s] + lane <= row_pos, base[2 * s + 1] + lane <= row_pos], 1
        )
        weights = jnp.where(causal, jnp.exp(jnp.where(causal, scores, 0.0)), 0.0)
        totals += jnp.sum(weights, 1, keepdims=True)
        mixed += jnp.dot(weights.astype(BF16), values, preferred_element_type=F32)
    attended = (mixed / totals).astype(BF16)
    for h in range(heads):
        out[:, h * HD : (h + 1) * HD] = attended[h * per_chunk : (h + 1) * per_chunk]


def stack_kernel(*refs):
    for s, ref in zip(STEPS, refs[:4]):
        refs[4][s] = ref[...]


def line_kernel(line, weight, out):
    rows, width = line.shape[1:]
    block = line[...].reshape(4 * rows, width)
    product = jnp.dot(block, weight[...], preferred_element_type=F32).astype(BF16)
    for s in range(4):
        out[s] = product[s * rows : (s + 1) * rows]


def output_kernel(place, *refs):
    early, line, weight, kept, sent, last, chunks = refs[:3], *refs[3:]
    line_kernel(line, weight, last)
    for t, part in zip(STEPS, [*early, last]):
        for s in range(4):
            chunks[chunk_at(place, place[0] ^ s, place[1] ^ t)] = part[s]
    half = kept.shape[0]
    kept[...] = chunks[:half]
    sent[...] = chunks[half:]


def chip_kernel(kept, got, *outs):
    rows = outs[0].shape[0]
    for s, out in enumerate(outs):
        part = slice(s * rows, (s + 1) * rows)
        out[...] = (kept[part, :].astype(F32) + got[part, :].astype(F32)).astype(BF16)


def call(kernel, outs, args, specs=(), scratch=()):
    specs = list(specs) + [VMEM] * (len(args) - len(specs))
    return pl.pallas_call(
        kernel,
        out_shape=[
            s if isinstance(s, jax.ShapeDtypeStruct) else jax.ShapeDtypeStruct(s, BF16)
            for s in outs
        ],
        in_specs=specs,
        out_specs=[VMEM] * len(outs),
        scratch_shapes=list(scratch),
        compiler_params=pltpu.CompilerParams(vmem_limit_bytes=32 * 1024 * 1024),
    )(*args)


def shards(tokens, w_query, w_keyval, w_output):
    zl = lax.axis_index("zl")
    core = lax.axis_index("core")
    y = lax.axis_index("y")
    x = lax.axis_index("x")
    per_row, features = tokens.shape
    half = per_row * Z_LO
    total = half * 2
    per_chunk = total // (Y * X)
    width = w_query.shape[1]
    heads = width // HD

    far = [partner(tokens, "zl", s) for s in FAR]

    def block_start(chip, side, index):
        return (((chip ^ (index & 3)) << 1) + ((index >> 2) ^ side)) * per_row

    chunk = y * X + x
    offset = (chunk & 1) * per_chunk
    source_chip, source_core = (zl >> 1) + 2 * core, zl & 1
    row_start = block_start(zl, core, chunk >> 1) + offset
    key_start = block_start(source_chip, source_core, chunk >> 1) + offset
    starts = [block_start(source_chip, source_core, i) for i in range(8)]
    base = jnp.stack([*starts, row_start, core]).astype(jnp.int32)
    steps = jnp.arange(per_chunk)
    cosine, sine_v = tables((row_start + steps).astype(F32), HD)
    key_cos, key_sin = tables((key_start + steps).astype(F32), HD)
    key_cos = jnp.where(core == 0, key_cos, 1.0)
    key_sin = jnp.where(core == 0, key_sin, 0.0)
    first, second = jnp.where(core == 0, x, y), jnp.where(core == 0, y, x)
    place = jnp.stack([first, second, 1 + 3 * core, 4 - 3 * core]).astype(jnp.int32)

    near = partner(tokens, "core", 1)
    early, early_kv = call(
        early_kernel,
        [(4, per_chunk, width), (4, per_chunk, HD)],
        [tokens, near, w_query, w_keyval],
    )
    *far, early = lax.optimization_barrier((*far, early))
    *parts, kv_parts = call(
        late_kernel,
        [(4, per_chunk, width)] * 4 + [(Y * X, per_chunk, HD)],
        [
            place,
            *far,
            *[partner(block, "core", 1) for block in far],
            w_query,
            w_keyval,
            early,
            early_kv,
        ],
        [SMEM],
        [pltpu.VMEM((Y * X, per_chunk, width), BF16)],
    )
    kv_parts = lax.all_to_all(kv_parts, PLANE, 0, 0, tiled=True)
    (kv,) = call(sum_kernel, [(per_chunk, HD)], [kv_parts])

    moves = [(e, 2 * (e % 4) + e // 4) for e in range(8)]
    here = lax.ppermute(kv, ROW, moves)
    across = lax.ppermute(
        kv, (*ROW, "zh"), [(2 * e + h, 2 * r + 1 - h) for e, r in moves for h in range(2)]
    )
    (kv_block,) = call(keys_kernel, [(Y * X, per_chunk, HD)], [here, across, key_cos, key_sin])
    kv_own = lax.all_to_all(kv_block, PLANE, 0, 0, tiled=True).reshape(total, HD)
    kv_other = partner(kv_own, "core", 1)

    got = [across_plane(parts[s], s, False) for s in STEPS[1:]]
    halves = call(
        halve_kernel,
        [jax.ShapeDtypeStruct((per_chunk, width), F32), *[(per_chunk, width)] * 3],
        [place, parts[0], *got],
        [SMEM],
    )
    got = [across_plane(halves[t], t, True) for t in STEPS[1:]]
    (own,) = call(join_kernel, [(per_chunk, width)], [halves[0], *got])
    got = partner(own, "zh", 1)

    (attended,) = call(
        functools.partial(attention_kernel, heads),
        [(per_chunk, width)],
        [base, own, got, cosine, sine_v, kv_own, kv_other],
        [SMEM],
        [pltpu.VMEM((heads * per_chunk, HD), BF16), pltpu.VMEM((2, total, HD), BF16)],
    )

    (line,) = call(
        stack_kernel,
        [(4, per_chunk, width)],
        [attended] + [across_plane(attended, s, False) for s in STEPS[1:]],
    )
    gathered = [across_plane(line, t, True) for t in STEPS[1:]]
    early = []
    for block in gathered:
        (done,) = call(line_kernel, [(4, per_chunk, features)], [line, w_output])
        line, done = lax.optimization_barrier((block, done))
        early.append(done)
    kept, sent = call(
        output_kernel,
        [(Y * X // 2, per_chunk, features)] * 2,
        [place, *early, line, w_output],
        [SMEM],
        [
            pltpu.VMEM((4, per_chunk, features), BF16),
            pltpu.VMEM((Y * X, per_chunk, features), BF16),
        ],
    )
    kept, sent = kept.reshape(half, features), sent.reshape(half, features)
    chip = call(chip_kernel, [(per_row, features)] * 4, [kept, partner(sent, "core", 1)])
    blocks = [chip[0]] + [partner(chip[s], "zl", s) for s in (3, 2, 1)]
    return functools.reduce(jnp.add, [b.astype(F32) for b in blocks]).astype(BF16)


def solution(mesh):
    fine = Mesh(
        mesh.devices.reshape(Z_LO, CORE, Z_HI, Y, X), ("zl", "core", "zh", "y", "x")
    )
    return jax.shard_map(
        shards,
        mesh=fine,
        in_specs=(P(ROW, COL), P(COL, ROW), P(COL, ROW), P(ROW, COL)),
        out_specs=P(ROW, COL),
        check_vma=False,
    )
```

```python
import functools
import math

import jax
import jax.numpy as jnp
from jax import lax
from jax.experimental import pallas as pl
from jax.experimental.pallas import tpu as pltpu
from jax.sharding import Mesh
from jax.sharding import PartitionSpec as P

HD = 128
Z_LO, CORE, Z_HI, Y, X = 4, 2, 2, 4, 4
ROW = ("zl", "core")
COL = ("zh", "y", "x")
PLANE = ("y", "x")
STEPS = (0, 1, 3, 2)
FAR = (2, 3, 1)
BF16 = jnp.bfloat16
F32 = jnp.float32
VMEM = pl.BlockSpec(memory_space=pltpu.VMEM)
SMEM = pl.BlockSpec(memory_space=pltpu.SMEM)


def tables(positions, width):
    half_width = width // 2
    frequency = 500000.0 ** (-(jnp.arange(half_width).astype(F32) * 2.0 / width))
    angle_v = positions[:, None] * frequency[None, :]
    cosine, sine_v = jnp.cos(angle_v), jnp.sin(angle_v)
    return jnp.concatenate([cosine, cosine], 1), jnp.concatenate([-sine_v, sine_v], 1)


def rotate(values_in, cosine, sine_v):
    return values_in * cosine + pltpu.roll(values_in, HD // 2, 1) * sine_v


def partner(block, axis, step):
    size = {"zl": Z_LO, "core": CORE, "zh": Z_HI, "y": Y, "x": X}[axis]
    return lax.ppermute(block, axis, [(i, i ^ step) for i in range(size)])


def across_plane(block, step, second):
    pairs = []
    for c in range(CORE):
        for y in range(Y):
            for x in range(X):
                along_x = (c == 0) != second
                to_y, to_x = (y, x ^ step) if along_x else (y ^ step, x)
                pairs.append(((c * Y + y) * X + x, (c * Y + to_y) * X + to_x))
    return lax.ppermute(block, ("core", *PLANE), pairs)


def project(block, weight, chunks, k):
    size = chunks.shape[1]
    product = jnp.dot(block[...], weight[...], preferred_element_type=F32).astype(BF16)
    for b in range(2):
        chunks[k + b] = product[b * size : (b + 1) * size]


def early_kernel(*refs):
    blocks, w_query, w_kv, out, keyvals = refs[:2], *refs[2:]
    for i, block in enumerate(blocks):
        project(block, w_query, out, 2 * i)
        project(block, w_kv, keyvals, 2 * i)


def fill(blocks, weight, early, chunks):
    for side in range(2):
        for b in range(2):
            chunks[8 * side + b] = early[2 * side + b]
        for i in range(3):
            project(blocks[3 * side + i], weight, chunks, 8 * side + 2 * FAR[i])


def keyval_kernel(*refs):
    fill(refs[:6], *refs[6:])


def query_kernel(place, *refs):
    outs, chunks = refs[8:12], refs[12]
    fill(refs[:6], refs[6], refs[7], chunks)
    for s in range(4):
        for j in range(4):
            outs[s][j] = chunks[chunk_at(place, place[0] ^ s, j)]


def chunk_at(place, first, second):
    return first * place[2] + second * place[3]


def halve_kernel(place, a, b, c, d, *outs):
    for t, out in enumerate(outs):
        j = place[1] ^ t
        total = a[j].astype(F32) + b[j].astype(F32) + c[j].astype(F32) + d[j].astype(F32)
        out[...] = total.astype(out.dtype)


def join_kernel(a, b, c, d, out):
    total = a[...] + b[...].astype(F32) + c[...].astype(F32) + d[...].astype(F32)
    out[...] = total.astype(BF16)


def total_kernel(a, b, c, d, out):
    total = a[...].astype(F32) + b[...].astype(F32) + c[...].astype(F32) + d[...].astype(F32)
    out[...] = total.astype(BF16)


def sum_kernel(parts, out):
    total = parts[0].astype(F32)
    for c in range(1, parts.shape[0]):
        total += parts[c].astype(F32)
    out[...] = total.astype(BF16)


def keys_kernel(a, b, cosine, sine_v, out):
    total = (a[...].astype(F32) + b[...].astype(F32)).astype(BF16).astype(F32)
    block = rotate(total, cosine[...], sine_v[...]).astype(BF16)
    for c in range(out.shape[0]):
        out[c] = block


def attention_kernel(
    heads, base, own, got, cosine, sine_v, kv_own, kv_other, out, queries, pair
):
    per_chunk = own.shape[0]
    pair[0] = kv_own[...]
    for s in range(4):
        part = slice(s * 2 * HD, (s + 1) * 2 * HD)
        pair[1, part, :] = kv_other[(s ^ 1) * 2 * HD : ((s ^ 1) + 1) * 2 * HD, :]
    for h in range(heads):
        cols = slice(h * HD, (h + 1) * HD)
        total = own[:, cols].astype(F32) + got[:, cols].astype(F32)
        queries[h * per_chunk : (h + 1) * per_chunk, :] = rotate(
            total, cosine[...], sine_v[...]
        ).astype(BF16)
    query = queries[...]
    core = base[9]
    rows = heads * per_chunk
    row_pos = base[8] + lax.broadcasted_iota(jnp.int32, (rows, HD), 0) % per_chunk
    lane = lax.broadcasted_iota(jnp.int32, (rows, HD), 1)
    score_scale = 1.0 / math.sqrt(HD)
    totals = jnp.zeros((rows, 1), F32)
    mixed = jnp.zeros((rows, HD), F32)
    for s in range(4):
        part = slice(s * 2 * HD, (s + 1) * 2 * HD)
        keys, values = pair[core, part, :], pair[1 - core, part, :]
        scores = (
            lax.dot_general(query, keys, (((1,), (1,)), ((), ())), preferred_element_type=F32)
            * score_scale
        )
        causal = jnp.concatenate(
            [base[2 * s] + lane <= row_pos, base[2 * s + 1] + lane <= row_pos], 1
        )
        weights = jnp.where(causal, jnp.exp(jnp.where(causal, scores, 0.0)), 0.0)
        totals += jnp.sum(weights, 1, keepdims=True)
        mixed += jnp.dot(weights.astype(BF16), values, preferred_element_type=F32)
    attended = (mixed / totals).astype(BF16)
    for h in range(heads):
        out[:, h * HD : (h + 1) * HD] = attended[h * per_chunk : (h + 1) * per_chunk]


def stack_kernel(*refs):
    for s, ref in zip(STEPS, refs[:4]):
        refs[4][s] = ref[...]


def line_kernel(line, weight, out):
    rows, width = line.shape[1:]
    block = line[...].reshape(4 * rows, width)
    product = jnp.dot(block, weight[...], preferred_element_type=F32).astype(BF16)
    for s in range(4):
        out[s] = product[s * rows : (s + 1) * rows]


def output_kernel(place, *refs):
    early, line, weight, kept, sent, last, chunks = refs[:3], *refs[3:]
    line_kernel(line, weight, last)
    for t, part in zip(STEPS, [*early, last]):
        for s in range(4):
            chunks[chunk_at(place, place[0] ^ s, place[1] ^ t)] = part[s]
    half = kept.shape[0]
    kept[...] = chunks[:half]
    sent[...] = chunks[half:]


def chip_kernel(kept, got, *outs):
    rows = outs[0].shape[0]
    for s, out in enumerate(outs):
        part = slice(s * rows, (s + 1) * rows)
        out[...] = (kept[part, :].astype(F32) + got[part, :].astype(F32)).astype(BF16)


def call(kernel, outs, args, specs=(), scratch=()):
    specs = list(specs) + [VMEM] * (len(args) - len(specs))
    return pl.pallas_call(
        kernel,
        out_shape=[
            s if isinstance(s, jax.ShapeDtypeStruct) else jax.ShapeDtypeStruct(s, BF16)
            for s in outs
        ],
        in_specs=specs,
        out_specs=[VMEM] * len(outs),
        scratch_shapes=list(scratch),
        compiler_params=pltpu.CompilerParams(vmem_limit_bytes=32 * 1024 * 1024),
    )(*args)


def shards(tokens, w_query, w_keyval, w_output):
    zl = lax.axis_index("zl")
    core = lax.axis_index("core")
    y = lax.axis_index("y")
    x = lax.axis_index("x")
    per_row, features = tokens.shape
    half = per_row * Z_LO
    total = half * 2
    per_chunk = total // (Y * X)
    width = w_query.shape[1]
    heads = width // HD

    far = [partner(tokens, "zl", s) for s in FAR]

    def block_start(chip, side, index):
        return (((chip ^ (index & 3)) << 1) + ((index >> 2) ^ side)) * per_row

    chunk = y * X + x
    offset = (chunk & 1) * per_chunk
    source_chip, source_core = (zl >> 1) + 2 * core, zl & 1
    row_start = block_start(zl, core, chunk >> 1) + offset
    key_start = block_start(source_chip, source_core, chunk >> 1) + offset
    starts = [block_start(source_chip, source_core, i) for i in range(8)]
    base = jnp.stack([*starts, row_start, core]).astype(jnp.int32)
    steps = jnp.arange(per_chunk)
    cosine, sine_v = tables((row_start + steps).astype(F32), HD)
    key_cos, key_sin = tables((key_start + steps).astype(F32), HD)
    key_cos = jnp.where(core == 0, key_cos, 1.0)
    key_sin = jnp.where(core == 0, key_sin, 0.0)
    first, second = jnp.where(core == 0, x, y), jnp.where(core == 0, y, x)
    place = jnp.stack([first, second, 1 + 3 * core, 4 - 3 * core]).astype(jnp.int32)

    near = partner(tokens, "core", 1)
    early, early_kv = call(
        early_kernel,
        [(4, per_chunk, width), (4, per_chunk, HD)],
        [tokens, near, w_query, w_keyval],
    )
    *far, early = lax.optimization_barrier((*far, early))
    far += [partner(block, "core", 1) for block in far]
    (kv_parts,) = call(
        keyval_kernel, [(Y * X, per_chunk, HD)], [*far, w_keyval, early_kv]
    )
    parts = call(
        query_kernel,
        [(4, per_chunk, width)] * 4,
        [place, *far, w_query, early],
        [SMEM],
        [pltpu.VMEM((Y * X, per_chunk, width), BF16)],
    )
    kv_parts = lax.all_to_all(kv_parts, PLANE, 0, 0, tiled=True)
    (kv,) = call(sum_kernel, [(per_chunk, HD)], [kv_parts])

    moves = [(e, 2 * (e % 4) + e // 4) for e in range(8)]
    here = lax.ppermute(kv, ROW, moves)
    across = lax.ppermute(
        kv, (*ROW, "zh"), [(2 * e + h, 2 * r + 1 - h) for e, r in moves for h in range(2)]
    )
    (kv_block,) = call(keys_kernel, [(Y * X, per_chunk, HD)], [here, across, key_cos, key_sin])
    got = [across_plane(parts[s], s, False) for s in STEPS[1:]]
    halves = call(
        halve_kernel,
        [jax.ShapeDtypeStruct((per_chunk, width), F32), *[(per_chunk, width)] * 3],
        [place, parts[0], *got],
        [SMEM],
    )
    got = [across_plane(halves[t], t, True) for t in STEPS[1:]]
    kv_own = lax.all_to_all(kv_block, PLANE, 0, 0, tiled=True).reshape(total, HD)
    kv_other = partner(kv_own, "core", 1)
    (own,) = call(join_kernel, [(per_chunk, width)], [halves[0], *got])
    got = partner(own, "zh", 1)

    (attended,) = call(
        functools.partial(attention_kernel, heads),
        [(per_chunk, width)],
        [base, own, got, cosine, sine_v, kv_own, kv_other],
        [SMEM],
        [pltpu.VMEM((heads * per_chunk, HD), BF16), pltpu.VMEM((2, total, HD), BF16)],
    )

    (line,) = call(
        stack_kernel,
        [(4, per_chunk, width)],
        [attended] + [across_plane(attended, s, False) for s in STEPS[1:]],
    )
    gathered = [across_plane(line, t, True) for t in STEPS[1:]]
    early = []
    for block in gathered:
        (done,) = call(line_kernel, [(4, per_chunk, features)], [line, w_output])
        line, done = lax.optimization_barrier((block, done))
        early.append(done)
    kept, sent = call(
        output_kernel,
        [(Y * X // 2, per_chunk, features)] * 2,
        [place, *early, line, w_output],
        [SMEM],
        [
            pltpu.VMEM((4, per_chunk, features), BF16),
            pltpu.VMEM((Y * X, per_chunk, features), BF16),
        ],
    )
    kept, sent = kept.reshape(half, features), sent.reshape(half, features)
    chip = call(chip_kernel, [(per_row, features)] * 4, [kept, partner(sent, "core", 1)])
    blocks = [chip[0]] + [partner(chip[s], "zl", s) for s in FAR]
    (result,) = call(total_kernel, [(per_row, features)], blocks)
    return result


def solution(mesh):
    fine = Mesh(
        mesh.devices.reshape(Z_LO, CORE, Z_HI, Y, X), ("zl", "core", "zh", "y", "x")
    )
    return jax.shard_map(
        shards,
        mesh=fine,
        in_specs=(P(ROW, COL), P(COL, ROW), P(COL, ROW), P(ROW, COL)),
        out_specs=P(ROW, COL),
        check_vma=False,
    )
```

```python
import functools
import math

import jax
import jax.numpy as jnp
from jax import lax
from jax.experimental import pallas as pl
from jax.experimental.pallas import tpu as pltpu
from jax.sharding import Mesh
from jax.sharding import PartitionSpec as P

HD = 128
Z_LO, CORE, Z_HI, Y, X = 4, 2, 2, 4, 4
ROW = ("zl", "core")
COL = ("zh", "y", "x")
PLANE = ("y", "x")
STEPS = (0, 1, 3, 2)
FAR = (2, 3, 1)
BF16 = jnp.bfloat16
F32 = jnp.float32
VMEM = pl.BlockSpec(memory_space=pltpu.VMEM)
SMEM = pl.BlockSpec(memory_space=pltpu.SMEM)


def tables(positions, width):
    half_width = width // 2
    frequency = 500000.0 ** (-(jnp.arange(half_width).astype(F32) * 2.0 / width))
    angle_v = positions[:, None] * frequency[None, :]
    cosine, sine_v = jnp.cos(angle_v), jnp.sin(angle_v)
    return jnp.concatenate([cosine, cosine], 1), jnp.concatenate([-sine_v, sine_v], 1)


def rotate(values_in, cosine, sine_v):
    return values_in * cosine + pltpu.roll(values_in, HD // 2, 1) * sine_v


def partner(block, axis, step):
    size = {"zl": Z_LO, "core": CORE, "zh": Z_HI, "y": Y, "x": X}[axis]
    return lax.ppermute(block, axis, [(i, i ^ step) for i in range(size)])


def across_plane(block, step, second):
    pairs = []
    for c in range(CORE):
        for y in range(Y):
            for x in range(X):
                along_x = (c == 0) != second
                to_y, to_x = (y, x ^ step) if along_x else (y ^ step, x)
                pairs.append(((c * Y + y) * X + x, (c * Y + to_y) * X + to_x))
    return lax.ppermute(block, ("core", *PLANE), pairs)


def project(block, weight, chunks, k):
    size = chunks.shape[1]
    product = jnp.dot(block[...], weight[...], preferred_element_type=F32).astype(BF16)
    for b in range(2):
        chunks[k + b] = product[b * size : (b + 1) * size]


def early_kernel(*refs):
    blocks, w_query, w_kv, out, keyvals = refs[:2], *refs[2:]
    for i, block in enumerate(blocks):
        project(block, w_query, out, 2 * i)
        project(block, w_kv, keyvals, 2 * i)


def fill(blocks, weight, early, chunks):
    for side in range(2):
        for b in range(2):
            chunks[8 * side + b] = early[2 * side + b]
        for i in range(3):
            project(blocks[3 * side + i], weight, chunks, 8 * side + 2 * FAR[i])


def keyval_kernel(*refs):
    fill(refs[:6], *refs[6:])


def query_kernel(place, *refs):
    outs, chunks = refs[8:12], refs[12]
    fill(refs[:6], refs[6], refs[7], chunks)
    for s in range(4):
        for j in range(4):
            outs[s][j] = chunks[chunk_at(place, place[0] ^ s, j)]


def chunk_at(place, first, second):
    return first * place[2] + second * place[3]


def halve_kernel(place, a, b, c, d, *outs):
    for t, out in enumerate(outs):
        j = place[1] ^ t
        total = a[j].astype(F32) + b[j].astype(F32) + c[j].astype(F32) + d[j].astype(F32)
        out[...] = total.astype(out.dtype)


def join_kernel(a, b, c, d, out):
    total = a[...] + b[...].astype(F32) + c[...].astype(F32) + d[...].astype(F32)
    out[...] = total.astype(BF16)


def total_kernel(a, b, c, d, out):
    total = a[...].astype(F32) + b[...].astype(F32) + c[...].astype(F32) + d[...].astype(F32)
    out[...] = total.astype(BF16)


def sum_kernel(parts, out):
    total = parts[0].astype(F32)
    for c in range(1, parts.shape[0]):
        total += parts[c].astype(F32)
    out[...] = total.astype(BF16)


def keys_kernel(a, b, cosine, sine_v, out):
    total = (a[...].astype(F32) + b[...].astype(F32)).astype(BF16).astype(F32)
    block = rotate(total, cosine[...], sine_v[...]).astype(BF16)
    for c in range(out.shape[0]):
        out[c] = block


def attention_kernel(
    heads, base, own, got, cosine, sine_v, kv_own, kv_other, out, queries, pair
):
    per_chunk = own.shape[0]
    pair[0] = kv_own[...]
    for s in range(4):
        part = slice(s * 2 * HD, (s + 1) * 2 * HD)
        pair[1, part, :] = kv_other[(s ^ 1) * 2 * HD : ((s ^ 1) + 1) * 2 * HD, :]
    for h in range(heads):
        cols = slice(h * HD, (h + 1) * HD)
        total = own[:, cols].astype(F32) + got[:, cols].astype(F32)
        queries[h * per_chunk : (h + 1) * per_chunk, :] = rotate(
            total, cosine[...], sine_v[...]
        ).astype(BF16)
    query = queries[...]
    core = base[9]
    rows = heads * per_chunk
    row_pos = base[8] + lax.broadcasted_iota(jnp.int32, (rows, HD), 0) % per_chunk
    lane = lax.broadcasted_iota(jnp.int32, (rows, HD), 1)
    score_scale = 1.0 / math.sqrt(HD)
    totals = jnp.zeros((rows, 1), F32)
    mixed = jnp.zeros((rows, HD), F32)
    for s in range(4):
        part = slice(s * 2 * HD, (s + 1) * 2 * HD)
        keys, values = pair[core, part, :], pair[1 - core, part, :]
        scores = (
            lax.dot_general(query, keys, (((1,), (1,)), ((), ())), preferred_element_type=F32)
            * score_scale
        )
        causal = jnp.concatenate(
            [base[2 * s] + lane <= row_pos, base[2 * s + 1] + lane <= row_pos], 1
        )
        weights = jnp.where(causal, jnp.exp(jnp.where(causal, scores, 0.0)), 0.0)
        totals += jnp.sum(weights, 1, keepdims=True)
        mixed += jnp.dot(weights.astype(BF16), values, preferred_element_type=F32)
    attended = (mixed / totals).astype(BF16)
    for h in range(heads):
        out[:, h * HD : (h + 1) * HD] = attended[h * per_chunk : (h + 1) * per_chunk]


def stack_kernel(*refs):
    for i, ref in enumerate(refs[:3]):
        refs[3][i] = ref[...]


def line_kernel(block, line, weight, out):
    rows, width = block.shape
    blocks = jnp.concatenate([block[...][None], line[...]], 0).reshape(4 * rows, width)
    product = jnp.dot(blocks, weight[...], preferred_element_type=F32).astype(BF16)
    for i in range(4):
        out[i] = product[i * rows : (i + 1) * rows]


def output_kernel(place, *refs):
    early, block, line, weight, kept, sent, last, chunks = refs[:3], *refs[3:]
    line_kernel(block, line, weight, last)
    for t, part in zip(STEPS, [*early, last]):
        for i, s in enumerate(STEPS):
            chunks[chunk_at(place, place[0] ^ s, place[1] ^ t)] = part[i]
    half = kept.shape[0]
    kept[...] = chunks[:half]
    sent[...] = chunks[half:]


def chip_kernel(kept, got, *outs):
    rows = outs[0].shape[0]
    for s, out in enumerate(outs):
        part = slice(s * rows, (s + 1) * rows)
        out[...] = (kept[part, :].astype(F32) + got[part, :].astype(F32)).astype(BF16)


def call(kernel, outs, args, specs=(), scratch=()):
    specs = list(specs) + [VMEM] * (len(args) - len(specs))
    return pl.pallas_call(
        kernel,
        out_shape=[
            s if isinstance(s, jax.ShapeDtypeStruct) else jax.ShapeDtypeStruct(s, BF16)
            for s in outs
        ],
        in_specs=specs,
        out_specs=[VMEM] * len(outs),
        scratch_shapes=list(scratch),
        compiler_params=pltpu.CompilerParams(vmem_limit_bytes=32 * 1024 * 1024),
    )(*args)


def shards(tokens, w_query, w_keyval, w_output):
    zl = lax.axis_index("zl")
    core = lax.axis_index("core")
    y = lax.axis_index("y")
    x = lax.axis_index("x")
    per_row, features = tokens.shape
    half = per_row * Z_LO
    total = half * 2
    per_chunk = total // (Y * X)
    width = w_query.shape[1]
    heads = width // HD

    far = [partner(tokens, "zl", s) for s in FAR]

    def block_start(chip, side, index):
        return (((chip ^ (index & 3)) << 1) + ((index >> 2) ^ side)) * per_row

    chunk = y * X + x
    offset = (chunk & 1) * per_chunk
    source_chip, source_core = (zl >> 1) + 2 * core, zl & 1
    row_start = block_start(zl, core, chunk >> 1) + offset
    key_start = block_start(source_chip, source_core, chunk >> 1) + offset
    starts = [block_start(source_chip, source_core, i) for i in range(8)]
    base = jnp.stack([*starts, row_start, core]).astype(jnp.int32)
    steps = jnp.arange(per_chunk)
    cosine, sine_v = tables((row_start + steps).astype(F32), HD)
    key_cos, key_sin = tables((key_start + steps).astype(F32), HD)
    key_cos = jnp.where(core == 0, key_cos, 1.0)
    key_sin = jnp.where(core == 0, key_sin, 0.0)
    first, second = jnp.where(core == 0, x, y), jnp.where(core == 0, y, x)
    place = jnp.stack([first, second, 1 + 3 * core, 4 - 3 * core]).astype(jnp.int32)

    near = partner(tokens, "core", 1)
    early, early_kv = call(
        early_kernel,
        [(4, per_chunk, width), (4, per_chunk, HD)],
        [tokens, near, w_query, w_keyval],
    )
    *far, early = lax.optimization_barrier((*far, early))
    far += [partner(block, "core", 1) for block in far]
    (kv_parts,) = call(
        keyval_kernel, [(Y * X, per_chunk, HD)], [*far, w_keyval, early_kv]
    )
    parts = call(
        query_kernel,
        [(4, per_chunk, width)] * 4,
        [place, *far, w_query, early],
        [SMEM],
        [pltpu.VMEM((Y * X, per_chunk, width), BF16)],
    )
    kv_parts = lax.all_to_all(kv_parts, PLANE, 0, 0, tiled=True)
    (kv,) = call(sum_kernel, [(per_chunk, HD)], [kv_parts])

    moves = [(e, 2 * (e % 4) + e // 4) for e in range(8)]
    here = lax.ppermute(kv, ROW, moves)
    across = lax.ppermute(
        kv, (*ROW, "zh"), [(2 * e + h, 2 * r + 1 - h) for e, r in moves for h in range(2)]
    )
    (kv_block,) = call(keys_kernel, [(Y * X, per_chunk, HD)], [here, across, key_cos, key_sin])
    got = [across_plane(parts[s], s, False) for s in STEPS[1:]]
    halves = call(
        halve_kernel,
        [jax.ShapeDtypeStruct((per_chunk, width), F32), *[(per_chunk, width)] * 3],
        [place, parts[0], *got],
        [SMEM],
    )
    got = [across_plane(halves[t], t, True) for t in STEPS[1:]]
    kv_own = lax.all_to_all(kv_block, PLANE, 0, 0, tiled=True).reshape(total, HD)
    kv_other = partner(kv_own, "core", 1)
    (own,) = call(join_kernel, [(per_chunk, width)], [halves[0], *got])
    got = partner(own, "zh", 1)

    (attended,) = call(
        functools.partial(attention_kernel, heads),
        [(per_chunk, width)],
        [base, own, got, cosine, sine_v, kv_own, kv_other],
        [SMEM],
        [pltpu.VMEM((heads * per_chunk, HD), BF16), pltpu.VMEM((2, total, HD), BF16)],
    )

    around = [across_plane(attended, s, False) for s in STEPS[1:]]
    direct = [across_plane(attended, t, True) for t in STEPS[1:]]
    around, direct = lax.optimization_barrier((around, direct))
    (line,) = call(stack_kernel, [(3, per_chunk, width)], around)
    gathered = [across_plane(line, t, True) for t in STEPS[1:]]
    early, block = [], attended
    for t in range(3):
        (done,) = call(line_kernel, [(4, per_chunk, features)], [block, line, w_output])
        line, done = lax.optimization_barrier((gathered[t], done))
        block = direct[t]
        early.append(done)
    kept, sent = call(
        output_kernel,
        [(Y * X // 2, per_chunk, features)] * 2,
        [place, *early, block, line, w_output],
        [SMEM],
        [
            pltpu.VMEM((4, per_chunk, features), BF16),
            pltpu.VMEM((Y * X, per_chunk, features), BF16),
        ],
    )
    kept, sent = kept.reshape(half, features), sent.reshape(half, features)
    chip = call(chip_kernel, [(per_row, features)] * 4, [kept, partner(sent, "core", 1)])
    blocks = [chip[0]] + [partner(chip[s], "zl", s) for s in FAR]
    (result,) = call(total_kernel, [(per_row, features)], blocks)
    return result


def solution(mesh):
    fine = Mesh(
        mesh.devices.reshape(Z_LO, CORE, Z_HI, Y, X), ("zl", "core", "zh", "y", "x")
    )
    return jax.shard_map(
        shards,
        mesh=fine,
        in_specs=(P(ROW, COL), P(COL, ROW), P(COL, ROW), P(ROW, COL)),
        out_specs=P(ROW, COL),
        check_vma=False,
    )
```

```python
import functools
import math

import jax
import jax.numpy as jnp
from jax import lax
from jax.experimental import pallas as pl
from jax.experimental.pallas import tpu as pltpu
from jax.sharding import Mesh
from jax.sharding import PartitionSpec as P

HD = 128
Z_LO, CORE, Z_HI, Y, X = 4, 2, 2, 4, 4
ROW = ("zl", "core")
COL = ("zh", "y", "x")
PLANE = ("y", "x")
STEPS = (0, 1, 3, 2)
FAR = (2, 3, 1)
BF16 = jnp.bfloat16
F32 = jnp.float32
VMEM = pl.BlockSpec(memory_space=pltpu.VMEM)
SMEM = pl.BlockSpec(memory_space=pltpu.SMEM)


def tables(positions, width):
    half_width = width // 2
    frequency = 500000.0 ** (-(jnp.arange(half_width).astype(F32) * 2.0 / width))
    angle_v = positions[:, None] * frequency[None, :]
    cosine, sine_v = jnp.cos(angle_v), jnp.sin(angle_v)
    return jnp.concatenate([cosine, cosine], 1), jnp.concatenate([-sine_v, sine_v], 1)


def rotate(values_in, cosine, sine_v):
    return values_in * cosine + pltpu.roll(values_in, HD // 2, 1) * sine_v


def partner(block, axis, step):
    size = {"zl": Z_LO, "core": CORE, "zh": Z_HI, "y": Y, "x": X}[axis]
    return lax.ppermute(block, axis, [(i, i ^ step) for i in range(size)])


def across_plane(block, step, second):
    pairs = []
    for c in range(CORE):
        for y in range(Y):
            for x in range(X):
                along_x = (c == 0) != second
                to_y, to_x = (y, x ^ step) if along_x else (y ^ step, x)
                pairs.append(((c * Y + y) * X + x, (c * Y + to_y) * X + to_x))
    return lax.ppermute(block, ("core", *PLANE), pairs)


def project(block, weight, chunks, k):
    size = chunks.shape[1]
    product = jnp.dot(block[...], weight[...], preferred_element_type=F32).astype(BF16)
    for b in range(2):
        chunks[k + b] = product[b * size : (b + 1) * size]


def early_kernel(*refs):
    blocks, w_query, w_kv, out, keyvals = refs[:2], *refs[2:]
    for i, block in enumerate(blocks):
        project(block, w_query, out, 2 * i)
        project(block, w_kv, keyvals, 2 * i)


def fill(blocks, weight, early, chunks):
    for side in range(2):
        for b in range(2):
            chunks[8 * side + b] = early[2 * side + b]
        for i in range(3):
            project(blocks[3 * side + i], weight, chunks, 8 * side + 2 * FAR[i])


def keyval_kernel(*refs):
    fill(refs[:6], *refs[6:])


def query_kernel(place, *refs):
    outs, chunks = refs[8:12], refs[12]
    fill(refs[:6], refs[6], refs[7], chunks)
    for s in range(4):
        for j in range(4):
            outs[s][j] = chunks[chunk_at(place, place[0] ^ s, j)]


def chunk_at(place, first, second):
    return first * place[2] + second * place[3]


def halve_kernel(place, a, b, c, d, *outs):
    for t, out in enumerate(outs):
        j = place[1] ^ t
        total = a[j].astype(F32) + b[j].astype(F32) + c[j].astype(F32) + d[j].astype(F32)
        out[...] = total.astype(out.dtype)


def join_kernel(a, b, c, d, out):
    total = a[...] + b[...].astype(F32) + c[...].astype(F32) + d[...].astype(F32)
    out[...] = total.astype(BF16)


def total_kernel(a, b, c, d, out):
    total = a[...].astype(F32) + b[...].astype(F32) + c[...].astype(F32) + d[...].astype(F32)
    out[...] = total.astype(BF16)


def sum_kernel(parts, out):
    total = parts[0].astype(F32)
    for c in range(1, parts.shape[0]):
        total += parts[c].astype(F32)
    out[...] = total.astype(BF16)


def keys_kernel(a, b, cosine, sine_v, out):
    total = (a[...].astype(F32) + b[...].astype(F32)).astype(BF16).astype(F32)
    block = rotate(total, cosine[...], sine_v[...]).astype(BF16)
    for c in range(out.shape[0]):
        out[c] = block


def attention_kernel(
    heads, base, own, got, cosine, sine_v, kv_own, kv_other, out, queries, pair
):
    per_chunk = own.shape[0]
    pair[0] = kv_own[...]
    for s in range(4):
        part = slice(s * 2 * HD, (s + 1) * 2 * HD)
        pair[1, part, :] = kv_other[(s ^ 1) * 2 * HD : ((s ^ 1) + 1) * 2 * HD, :]
    for h in range(heads):
        cols = slice(h * HD, (h + 1) * HD)
        total = own[:, cols].astype(F32) + got[:, cols].astype(F32)
        queries[h * per_chunk : (h + 1) * per_chunk, :] = rotate(
            total, cosine[...], sine_v[...]
        ).astype(BF16)
    query = queries[...]
    core = base[9]
    rows = heads * per_chunk
    row_pos = base[8] + lax.broadcasted_iota(jnp.int32, (rows, HD), 0) % per_chunk
    lane = lax.broadcasted_iota(jnp.int32, (rows, HD), 1)
    score_scale = 1.0 / math.sqrt(HD)
    totals = jnp.zeros((rows, 1), F32)
    mixed = jnp.zeros((rows, HD), F32)
    for s in range(4):
        part = slice(s * 2 * HD, (s + 1) * 2 * HD)
        keys, values = pair[core, part, :], pair[1 - core, part, :]
        scores = (
            lax.dot_general(query, keys, (((1,), (1,)), ((), ())), preferred_element_type=F32)
            * score_scale
        )
        causal = jnp.concatenate(
            [base[2 * s] + lane <= row_pos, base[2 * s + 1] + lane <= row_pos], 1
        )
        weights = jnp.where(causal, jnp.exp(jnp.where(causal, scores, 0.0)), 0.0)
        totals += jnp.sum(weights, 1, keepdims=True)
        mixed += jnp.dot(weights.astype(BF16), values, preferred_element_type=F32)
    attended = (mixed / totals).astype(BF16)
    for h in range(heads):
        out[:, h * HD : (h + 1) * HD] = attended[h * per_chunk : (h + 1) * per_chunk]


def stack_kernel(*refs):
    for s, ref in zip(STEPS, refs[:4]):
        refs[4][s] = ref[...]


def line_kernel(line, weight, out):
    rows, width = line.shape[1:]
    block = line[...].reshape(4 * rows, width)
    product = jnp.dot(block, weight[...], preferred_element_type=F32).astype(BF16)
    for s in range(4):
        out[s] = product[s * rows : (s + 1) * rows]


def output_kernel(place, *refs):
    early, line, weight, kept, sent, last, chunks = refs[:3], *refs[3:]
    line_kernel(line, weight, last)
    for t, part in zip(STEPS, [*early, last]):
        for s in range(4):
            chunks[chunk_at(place, place[0] ^ s, place[1] ^ t)] = part[s]
    half = kept.shape[0]
    kept[...] = chunks[:half]
    sent[...] = chunks[half:]


def chip_kernel(kept, got, *outs):
    rows = outs[0].shape[0]
    for s, out in enumerate(outs):
        part = slice(s * rows, (s + 1) * rows)
        out[...] = (kept[part, :].astype(F32) + got[part, :].astype(F32)).astype(BF16)


def call(kernel, outs, args, specs=(), scratch=()):
    specs = list(specs) + [VMEM] * (len(args) - len(specs))
    return pl.pallas_call(
        kernel,
        out_shape=[
            s if isinstance(s, jax.ShapeDtypeStruct) else jax.ShapeDtypeStruct(s, BF16)
            for s in outs
        ],
        in_specs=specs,
        out_specs=[VMEM] * len(outs),
        scratch_shapes=list(scratch),
        compiler_params=pltpu.CompilerParams(vmem_limit_bytes=32 * 1024 * 1024),
    )(*args)


def shards(tokens, w_query, w_keyval, w_output):
    zl = lax.axis_index("zl")
    core = lax.axis_index("core")
    y = lax.axis_index("y")
    x = lax.axis_index("x")
    per_row, features = tokens.shape
    half = per_row * Z_LO
    total = half * 2
    per_chunk = total // (Y * X)
    width = w_query.shape[1]
    heads = width // HD

    far = [partner(tokens, "zl", s) for s in FAR]

    def block_start(chip, side, index):
        return (((chip ^ (index & 3)) << 1) + ((index >> 2) ^ side)) * per_row

    chunk = y * X + x
    offset = (chunk & 1) * per_chunk
    source_chip, source_core = (zl >> 1) + 2 * core, zl & 1
    row_start = block_start(zl, core, chunk >> 1) + offset
    key_start = block_start(source_chip, source_core, chunk >> 1) + offset
    starts = [block_start(source_chip, source_core, i) for i in range(8)]
    base = jnp.stack([*starts, row_start, core]).astype(jnp.int32)
    steps = jnp.arange(per_chunk)
    cosine, sine_v = tables((row_start + steps).astype(F32), HD)
    key_cos, key_sin = tables((key_start + steps).astype(F32), HD)
    key_cos = jnp.where(core == 0, key_cos, 1.0)
    key_sin = jnp.where(core == 0, key_sin, 0.0)
    first, second = jnp.where(core == 0, x, y), jnp.where(core == 0, y, x)
    place = jnp.stack([first, second, 1 + 3 * core, 4 - 3 * core]).astype(jnp.int32)

    near = partner(tokens, "core", 1)
    early, early_kv = call(
        early_kernel,
        [(4, per_chunk, width), (4, per_chunk, HD)],
        [tokens, near, w_query, w_keyval],
    )
    *far, early = lax.optimization_barrier((*far, early))
    far += [partner(block, "core", 1) for block in far]
    (kv_parts,) = call(
        keyval_kernel, [(Y * X, per_chunk, HD)], [*far, w_keyval, early_kv]
    )
    parts = call(
        query_kernel,
        [(4, per_chunk, width)] * 4,
        [place, *far, w_query, early],
        [SMEM],
        [pltpu.VMEM((Y * X, per_chunk, width), BF16)],
    )
    kv_parts = lax.all_to_all(kv_parts, PLANE, 0, 0, tiled=True)
    (kv,) = call(sum_kernel, [(per_chunk, HD)], [kv_parts])

    moves = [(e, 2 * (e % 4) + e // 4) for e in range(8)]
    across = lax.ppermute(
        kv, (*ROW, "zh"), [(2 * e + h, 2 * r + 1 - h) for e, r in moves for h in range(2)]
    )
    here = lax.ppermute(kv, ROW, moves)
    (kv_block,) = call(keys_kernel, [(Y * X, per_chunk, HD)], [across, here, key_cos, key_sin])
    got = [across_plane(parts[s], s, False) for s in STEPS[1:]]
    halves = call(
        halve_kernel,
        [jax.ShapeDtypeStruct((per_chunk, width), F32), *[(per_chunk, width)] * 3],
        [place, parts[0], *got],
        [SMEM],
    )
    got = [across_plane(halves[t], t, True) for t in STEPS[1:]]
    kv_own = lax.all_to_all(kv_block, PLANE, 0, 0, tiled=True).reshape(total, HD)
    kv_other = partner(kv_own, "core", 1)
    (own,) = call(join_kernel, [(per_chunk, width)], [halves[0], *got])
    got = partner(own, "zh", 1)

    (attended,) = call(
        functools.partial(attention_kernel, heads),
        [(per_chunk, width)],
        [base, own, got, cosine, sine_v, kv_own, kv_other],
        [SMEM],
        [pltpu.VMEM((heads * per_chunk, HD), BF16), pltpu.VMEM((2, total, HD), BF16)],
    )

    (line,) = call(
        stack_kernel,
        [(4, per_chunk, width)],
        [attended] + [across_plane(attended, s, False) for s in STEPS[1:]],
    )
    gathered = [across_plane(line, t, True) for t in STEPS[1:]]
    early = []
    for block in gathered:
        (done,) = call(line_kernel, [(4, per_chunk, features)], [line, w_output])
        line, done = lax.optimization_barrier((block, done))
        early.append(done)
    kept, sent = call(
        output_kernel,
        [(Y * X // 2, per_chunk, features)] * 2,
        [place, *early, line, w_output],
        [SMEM],
        [
            pltpu.VMEM((4, per_chunk, features), BF16),
            pltpu.VMEM((Y * X, per_chunk, features), BF16),
        ],
    )
    kept, sent = kept.reshape(half, features), sent.reshape(half, features)
    chip = call(chip_kernel, [(per_row, features)] * 4, [kept, partner(sent, "core", 1)])
    blocks = [chip[0]] + [partner(chip[s], "zl", s) for s in FAR]
    (result,) = call(total_kernel, [(per_row, features)], blocks)
    return result


def solution(mesh):
    fine = Mesh(
        mesh.devices.reshape(Z_LO, CORE, Z_HI, Y, X), ("zl", "core", "zh", "y", "x")
    )
    return jax.shard_map(
        shards,
        mesh=fine,
        in_specs=(P(ROW, COL), P(COL, ROW), P(COL, ROW), P(ROW, COL)),
        out_specs=P(ROW, COL),
        check_vma=False,
    )
```

```python
import functools
import math

import jax
import jax.numpy as jnp
from jax import lax
from jax.experimental import pallas as pl
from jax.experimental.pallas import tpu as pltpu
from jax.sharding import Mesh
from jax.sharding import PartitionSpec as P

HD = 128
Z_LO, CORE, Z_HI, Y, X = 4, 2, 2, 4, 4
ROW = ("zl", "core")
COL = ("zh", "y", "x")
PLANE = ("y", "x")
STEPS = (0, 1, 3, 2)
FAR = (3, 2, 1)
BF16 = jnp.bfloat16
F32 = jnp.float32
VMEM = pl.BlockSpec(memory_space=pltpu.VMEM)
SMEM = pl.BlockSpec(memory_space=pltpu.SMEM)


def tables(positions, width):
    half_width = width // 2
    frequency = 500000.0 ** (-(jnp.arange(half_width).astype(F32) * 2.0 / width))
    angle_v = positions[:, None] * frequency[None, :]
    cosine, sine_v = jnp.cos(angle_v), jnp.sin(angle_v)
    return jnp.concatenate([cosine, cosine], 1), jnp.concatenate([-sine_v, sine_v], 1)


def rotate(values_in, cosine, sine_v):
    return values_in * cosine + pltpu.roll(values_in, HD // 2, 1) * sine_v


def partner(block, axis, step):
    size = {"zl": Z_LO, "core": CORE, "zh": Z_HI, "y": Y, "x": X}[axis]
    return lax.ppermute(block, axis, [(i, i ^ step) for i in range(size)])


def across_plane(block, step, second):
    pairs = []
    for c in range(CORE):
        for y in range(Y):
            for x in range(X):
                along_x = (c == 0) != second
                to_y, to_x = (y, x ^ step) if along_x else (y ^ step, x)
                pairs.append(((c * Y + y) * X + x, (c * Y + to_y) * X + to_x))
    return lax.ppermute(block, ("core", *PLANE), pairs)


def project(block, weight, chunks, k):
    size = chunks.shape[1]
    product = jnp.dot(block[...], weight[...], preferred_element_type=F32).astype(BF16)
    for b in range(2):
        chunks[k + b] = product[b * size : (b + 1) * size]


def early_kernel(*refs):
    blocks, w_query, w_kv, out, keyvals = refs[:2], *refs[2:]
    for i, block in enumerate(blocks):
        project(block, w_query, out, 2 * i)
        project(block, w_kv, keyvals, 2 * i)


def fill(blocks, weight, early, chunks):
    for side in range(2):
        for b in range(2):
            chunks[8 * side + b] = early[2 * side + b]
        for i in range(3):
            project(blocks[3 * side + i], weight, chunks, 8 * side + 2 * FAR[i])


def keyval_kernel(*refs):
    fill(refs[:6], *refs[6:])


def query_kernel(place, *refs):
    outs, chunks = refs[8:12], refs[12]
    fill(refs[:6], refs[6], refs[7], chunks)
    for s in range(4):
        for j in range(4):
            outs[s][j] = chunks[chunk_at(place, place[0] ^ s, j)]


def chunk_at(place, first, second):
    return first * place[2] + second * place[3]


def halve_kernel(place, a, b, c, d, *outs):
    for t, out in enumerate(outs):
        j = place[1] ^ t
        total = a[j].astype(F32) + b[j].astype(F32) + c[j].astype(F32) + d[j].astype(F32)
        out[...] = total.astype(out.dtype)


def join_kernel(a, b, c, d, out):
    total = a[...] + b[...].astype(F32) + c[...].astype(F32) + d[...].astype(F32)
    out[...] = total.astype(BF16)


def total_kernel(a, b, c, d, out):
    total = a[...].astype(F32) + b[...].astype(F32) + c[...].astype(F32) + d[...].astype(F32)
    out[...] = total.astype(BF16)


def sum_kernel(parts, out):
    total = parts[0].astype(F32)
    for c in range(1, parts.shape[0]):
        total += parts[c].astype(F32)
    out[...] = total.astype(BF16)


def keys_kernel(a, b, cosine, sine_v, out):
    total = (a[...].astype(F32) + b[...].astype(F32)).astype(BF16).astype(F32)
    block = rotate(total, cosine[...], sine_v[...]).astype(BF16)
    for c in range(out.shape[0]):
        out[c] = block


def attention_kernel(
    heads, base, own, got, cosine, sine_v, kv_own, kv_other, out, queries, pair
):
    per_chunk = own.shape[0]
    pair[0] = kv_own[...]
    for s in range(4):
        part = slice(s * 2 * HD, (s + 1) * 2 * HD)
        pair[1, part, :] = kv_other[(s ^ 1) * 2 * HD : ((s ^ 1) + 1) * 2 * HD, :]
    for h in range(heads):
        cols = slice(h * HD, (h + 1) * HD)
        total = own[:, cols].astype(F32) + got[:, cols].astype(F32)
        queries[h * per_chunk : (h + 1) * per_chunk, :] = rotate(
            total, cosine[...], sine_v[...]
        ).astype(BF16)
    query = queries[...]
    core = base[9]
    rows = heads * per_chunk
    row_pos = base[8] + lax.broadcasted_iota(jnp.int32, (rows, HD), 0) % per_chunk
    lane = lax.broadcasted_iota(jnp.int32, (rows, HD), 1)
    score_scale = 1.0 / math.sqrt(HD)
    totals = jnp.zeros((rows, 1), F32)
    mixed = jnp.zeros((rows, HD), F32)
    for s in range(4):
        part = slice(s * 2 * HD, (s + 1) * 2 * HD)
        keys, values = pair[core, part, :], pair[1 - core, part, :]
        scores = (
            lax.dot_general(query, keys, (((1,), (1,)), ((), ())), preferred_element_type=F32)
            * score_scale
        )
        causal = jnp.concatenate(
            [base[2 * s] + lane <= row_pos, base[2 * s + 1] + lane <= row_pos], 1
        )
        weights = jnp.where(causal, jnp.exp(jnp.where(causal, scores, 0.0)), 0.0)
        totals += jnp.sum(weights, 1, keepdims=True)
        mixed += jnp.dot(weights.astype(BF16), values, preferred_element_type=F32)
    attended = (mixed / totals).astype(BF16)
    for h in range(heads):
        out[:, h * HD : (h + 1) * HD] = attended[h * per_chunk : (h + 1) * per_chunk]


def stack_kernel(*refs):
    for s, ref in zip(STEPS, refs[:4]):
        refs[4][s] = ref[...]


def line_kernel(line, weight, out):
    rows, width = line.shape[1:]
    block = line[...].reshape(4 * rows, width)
    product = jnp.dot(block, weight[...], preferred_element_type=F32).astype(BF16)
    for s in range(4):
        out[s] = product[s * rows : (s + 1) * rows]


def output_kernel(place, *refs):
    early, line, weight, kept, sent, last, chunks = refs[:3], *refs[3:]
    line_kernel(line, weight, last)
    for t, part in zip(STEPS, [*early, last]):
        for s in range(4):
            chunks[chunk_at(place, place[0] ^ s, place[1] ^ t)] = part[s]
    half = kept.shape[0]
    kept[...] = chunks[:half]
    sent[...] = chunks[half:]


def chip_kernel(kept, got, *outs):
    rows = outs[0].shape[0]
    for s, out in enumerate(outs):
        part = slice(s * rows, (s + 1) * rows)
        out[...] = (kept[part, :].astype(F32) + got[part, :].astype(F32)).astype(BF16)


def call(kernel, outs, args, specs=(), scratch=()):
    specs = list(specs) + [VMEM] * (len(args) - len(specs))
    return pl.pallas_call(
        kernel,
        out_shape=[
            s if isinstance(s, jax.ShapeDtypeStruct) else jax.ShapeDtypeStruct(s, BF16)
            for s in outs
        ],
        in_specs=specs,
        out_specs=[VMEM] * len(outs),
        scratch_shapes=list(scratch),
        compiler_params=pltpu.CompilerParams(vmem_limit_bytes=32 * 1024 * 1024),
    )(*args)


def shards(tokens, w_query, w_keyval, w_output):
    zl = lax.axis_index("zl")
    core = lax.axis_index("core")
    y = lax.axis_index("y")
    x = lax.axis_index("x")
    per_row, features = tokens.shape
    half = per_row * Z_LO
    total = half * 2
    per_chunk = total // (Y * X)
    width = w_query.shape[1]
    heads = width // HD

    far = [partner(tokens, "zl", s) for s in FAR]

    def block_start(chip, side, index):
        return (((chip ^ (index & 3)) << 1) + ((index >> 2) ^ side)) * per_row

    chunk = y * X + x
    offset = (chunk & 1) * per_chunk
    source_chip, source_core = (zl >> 1) + 2 * core, zl & 1
    row_start = block_start(zl, core, chunk >> 1) + offset
    key_start = block_start(source_chip, source_core, chunk >> 1) + offset
    starts = [block_start(source_chip, source_core, i) for i in range(8)]
    base = jnp.stack([*starts, row_start, core]).astype(jnp.int32)
    steps = jnp.arange(per_chunk)
    cosine, sine_v = tables((row_start + steps).astype(F32), HD)
    key_cos, key_sin = tables((key_start + steps).astype(F32), HD)
    key_cos = jnp.where(core == 0, key_cos, 1.0)
    key_sin = jnp.where(core == 0, key_sin, 0.0)
    first, second = jnp.where(core == 0, x, y), jnp.where(core == 0, y, x)
    place = jnp.stack([first, second, 1 + 3 * core, 4 - 3 * core]).astype(jnp.int32)

    near = partner(tokens, "core", 1)
    early, early_kv = call(
        early_kernel,
        [(4, per_chunk, width), (4, per_chunk, HD)],
        [tokens, near, w_query, w_keyval],
    )
    *far, early = lax.optimization_barrier((*far, early))
    far += [partner(block, "core", 1) for block in far]
    (kv_parts,) = call(
        keyval_kernel, [(Y * X, per_chunk, HD)], [*far, w_keyval, early_kv]
    )
    parts = call(
        query_kernel,
        [(4, per_chunk, width)] * 4,
        [place, *far, w_query, early],
        [SMEM],
        [pltpu.VMEM((Y * X, per_chunk, width), BF16)],
    )
    kv_parts = lax.all_to_all(kv_parts, PLANE, 0, 0, tiled=True)
    (kv,) = call(sum_kernel, [(per_chunk, HD)], [kv_parts])

    moves = [(e, 2 * (e % 4) + e // 4) for e in range(8)]
    here = lax.ppermute(kv, ROW, moves)
    across = lax.ppermute(
        kv, (*ROW, "zh"), [(2 * e + h, 2 * r + 1 - h) for e, r in moves for h in range(2)]
    )
    (kv_block,) = call(keys_kernel, [(Y * X, per_chunk, HD)], [here, across, key_cos, key_sin])
    got = [across_plane(parts[s], s, False) for s in STEPS[1:]]
    halves = call(
        halve_kernel,
        [jax.ShapeDtypeStruct((per_chunk, width), F32), *[(per_chunk, width)] * 3],
        [place, parts[0], *got],
        [SMEM],
    )
    got = [across_plane(halves[t], t, True) for t in STEPS[1:]]
    kv_own = lax.all_to_all(kv_block, PLANE, 0, 0, tiled=True).reshape(total, HD)
    kv_other = partner(kv_own, "core", 1)
    (own,) = call(join_kernel, [(per_chunk, width)], [halves[0], *got])
    got = partner(own, "zh", 1)

    (attended,) = call(
        functools.partial(attention_kernel, heads),
        [(per_chunk, width)],
        [base, own, got, cosine, sine_v, kv_own, kv_other],
        [SMEM],
        [pltpu.VMEM((heads * per_chunk, HD), BF16), pltpu.VMEM((2, total, HD), BF16)],
    )

    (line,) = call(
        stack_kernel,
        [(4, per_chunk, width)],
        [attended] + [across_plane(attended, s, False) for s in STEPS[1:]],
    )
    gathered = [across_plane(line, t, True) for t in STEPS[1:]]
    early = []
    for block in gathered:
        (done,) = call(line_kernel, [(4, per_chunk, features)], [line, w_output])
        line, done = lax.optimization_barrier((block, done))
        early.append(done)
    kept, sent = call(
        output_kernel,
        [(Y * X // 2, per_chunk, features)] * 2,
        [place, *early, line, w_output],
        [SMEM],
        [
            pltpu.VMEM((4, per_chunk, features), BF16),
            pltpu.VMEM((Y * X, per_chunk, features), BF16),
        ],
    )
    kept, sent = kept.reshape(half, features), sent.reshape(half, features)
    chip = call(chip_kernel, [(per_row, features)] * 4, [kept, partner(sent, "core", 1)])
    blocks = [chip[0]] + [partner(chip[s], "zl", s) for s in FAR]
    (result,) = call(total_kernel, [(per_row, features)], blocks)
    return result


def solution(mesh):
    fine = Mesh(
        mesh.devices.reshape(Z_LO, CORE, Z_HI, Y, X), ("zl", "core", "zh", "y", "x")
    )
    return jax.shard_map(
        shards,
        mesh=fine,
        in_specs=(P(ROW, COL), P(COL, ROW), P(COL, ROW), P(ROW, COL)),
        out_specs=P(ROW, COL),
        check_vma=False,
    )
```

```python
import functools
import math

import jax
import jax.numpy as jnp
from jax import lax
from jax.experimental import pallas as pl
from jax.experimental.pallas import tpu as pltpu
from jax.sharding import Mesh
from jax.sharding import PartitionSpec as P

HD = 128
Z_LO, CORE, Z_HI, Y, X = 4, 2, 2, 4, 4
ROW = ("zl", "core")
COL = ("zh", "y", "x")
PLANE = ("y", "x")
STEPS = (0, 3, 1, 2)
FAR = (2, 3, 1)
BF16 = jnp.bfloat16
F32 = jnp.float32
VMEM = pl.BlockSpec(memory_space=pltpu.VMEM)
SMEM = pl.BlockSpec(memory_space=pltpu.SMEM)


def tables(positions, width):
    half_width = width // 2
    frequency = 500000.0 ** (-(jnp.arange(half_width).astype(F32) * 2.0 / width))
    angle_v = positions[:, None] * frequency[None, :]
    cosine, sine_v = jnp.cos(angle_v), jnp.sin(angle_v)
    return jnp.concatenate([cosine, cosine], 1), jnp.concatenate([-sine_v, sine_v], 1)


def rotate(values_in, cosine, sine_v):
    return values_in * cosine + pltpu.roll(values_in, HD // 2, 1) * sine_v


def partner(block, axis, step):
    size = {"zl": Z_LO, "core": CORE, "zh": Z_HI, "y": Y, "x": X}[axis]
    return lax.ppermute(block, axis, [(i, i ^ step) for i in range(size)])


def across_plane(block, step, second):
    pairs = []
    for c in range(CORE):
        for y in range(Y):
            for x in range(X):
                along_x = (c == 0) != second
                to_y, to_x = (y, x ^ step) if along_x else (y ^ step, x)
                pairs.append(((c * Y + y) * X + x, (c * Y + to_y) * X + to_x))
    return lax.ppermute(block, ("core", *PLANE), pairs)


def project(block, weight, chunks, k):
    size = chunks.shape[1]
    product = jnp.dot(block[...], weight[...], preferred_element_type=F32).astype(BF16)
    for b in range(2):
        chunks[k + b] = product[b * size : (b + 1) * size]


def early_kernel(*refs):
    blocks, w_query, w_kv, out, keyvals = refs[:2], *refs[2:]
    for i, block in enumerate(blocks):
        project(block, w_query, out, 2 * i)
        project(block, w_kv, keyvals, 2 * i)


def fill(blocks, weight, early, chunks):
    for side in range(2):
        for b in range(2):
            chunks[8 * side + b] = early[2 * side + b]
        for i in range(3):
            project(blocks[3 * side + i], weight, chunks, 8 * side + 2 * FAR[i])


def keyval_kernel(*refs):
    fill(refs[:6], *refs[6:])


def query_kernel(place, *refs):
    outs, chunks = refs[8:12], refs[12]
    fill(refs[:6], refs[6], refs[7], chunks)
    for s in range(4):
        for j in range(4):
            outs[s][j] = chunks[chunk_at(place, place[0] ^ s, j)]


def chunk_at(place, first, second):
    return first * place[2] + second * place[3]


def halve_kernel(place, a, b, c, d, *outs):
    for t, out in enumerate(outs):
        j = place[1] ^ t
        total = a[j].astype(F32) + b[j].astype(F32) + c[j].astype(F32) + d[j].astype(F32)
        out[...] = total.astype(out.dtype)


def join_kernel(a, b, c, d, out):
    total = a[...] + b[...].astype(F32) + c[...].astype(F32) + d[...].astype(F32)
    out[...] = total.astype(BF16)


def total_kernel(a, b, c, d, out):
    total = a[...].astype(F32) + b[...].astype(F32) + c[...].astype(F32) + d[...].astype(F32)
    out[...] = total.astype(BF16)


def sum_kernel(parts, out):
    total = parts[0].astype(F32)
    for c in range(1, parts.shape[0]):
        total += parts[c].astype(F32)
    out[...] = total.astype(BF16)


def keys_kernel(a, b, cosine, sine_v, out):
    total = (a[...].astype(F32) + b[...].astype(F32)).astype(BF16).astype(F32)
    block = rotate(total, cosine[...], sine_v[...]).astype(BF16)
    for c in range(out.shape[0]):
        out[c] = block


def attention_kernel(
    heads, base, own, got, cosine, sine_v, kv_own, kv_other, out, queries, pair
):
    per_chunk = own.shape[0]
    pair[0] = kv_own[...]
    for s in range(4):
        part = slice(s * 2 * HD, (s + 1) * 2 * HD)
        pair[1, part, :] = kv_other[(s ^ 1) * 2 * HD : ((s ^ 1) + 1) * 2 * HD, :]
    for h in range(heads):
        cols = slice(h * HD, (h + 1) * HD)
        total = own[:, cols].astype(F32) + got[:, cols].astype(F32)
        queries[h * per_chunk : (h + 1) * per_chunk, :] = rotate(
            total, cosine[...], sine_v[...]
        ).astype(BF16)
    query = queries[...]
    core = base[9]
    rows = heads * per_chunk
    row_pos = base[8] + lax.broadcasted_iota(jnp.int32, (rows, HD), 0) % per_chunk
    lane = lax.broadcasted_iota(jnp.int32, (rows, HD), 1)
    score_scale = 1.0 / math.sqrt(HD)
    totals = jnp.zeros((rows, 1), F32)
    mixed = jnp.zeros((rows, HD), F32)
    for s in range(4):
        part = slice(s * 2 * HD, (s + 1) * 2 * HD)
        keys, values = pair[core, part, :], pair[1 - core, part, :]
        scores = (
            lax.dot_general(query, keys, (((1,), (1,)), ((), ())), preferred_element_type=F32)
            * score_scale
        )
        causal = jnp.concatenate(
            [base[2 * s] + lane <= row_pos, base[2 * s + 1] + lane <= row_pos], 1
        )
        weights = jnp.where(causal, jnp.exp(jnp.where(causal, scores, 0.0)), 0.0)
        totals += jnp.sum(weights, 1, keepdims=True)
        mixed += jnp.dot(weights.astype(BF16), values, preferred_element_type=F32)
    attended = (mixed / totals).astype(BF16)
    for h in range(heads):
        out[:, h * HD : (h + 1) * HD] = attended[h * per_chunk : (h + 1) * per_chunk]


def stack_kernel(*refs):
    for s, ref in zip(STEPS, refs[:4]):
        refs[4][s] = ref[...]


def line_kernel(line, weight, out):
    rows, width = line.shape[1:]
    block = line[...].reshape(4 * rows, width)
    product = jnp.dot(block, weight[...], preferred_element_type=F32).astype(BF16)
    for s in range(4):
        out[s] = product[s * rows : (s + 1) * rows]


def output_kernel(place, *refs):
    early, line, weight, kept, sent, last, chunks = refs[:3], *refs[3:]
    line_kernel(line, weight, last)
    for t, part in zip(STEPS, [*early, last]):
        for s in range(4):
            chunks[chunk_at(place, place[0] ^ s, place[1] ^ t)] = part[s]
    half = kept.shape[0]
    kept[...] = chunks[:half]
    sent[...] = chunks[half:]


def chip_kernel(kept, got, *outs):
    rows = outs[0].shape[0]
    for s, out in enumerate(outs):
        part = slice(s * rows, (s + 1) * rows)
        out[...] = (kept[part, :].astype(F32) + got[part, :].astype(F32)).astype(BF16)


def call(kernel, outs, args, specs=(), scratch=()):
    specs = list(specs) + [VMEM] * (len(args) - len(specs))
    return pl.pallas_call(
        kernel,
        out_shape=[
            s if isinstance(s, jax.ShapeDtypeStruct) else jax.ShapeDtypeStruct(s, BF16)
            for s in outs
        ],
        in_specs=specs,
        out_specs=[VMEM] * len(outs),
        scratch_shapes=list(scratch),
        compiler_params=pltpu.CompilerParams(vmem_limit_bytes=32 * 1024 * 1024),
    )(*args)


def shards(tokens, w_query, w_keyval, w_output):
    zl = lax.axis_index("zl")
    core = lax.axis_index("core")
    y = lax.axis_index("y")
    x = lax.axis_index("x")
    per_row, features = tokens.shape
    half = per_row * Z_LO
    total = half * 2
    per_chunk = total // (Y * X)
    width = w_query.shape[1]
    heads = width // HD

    far = [partner(tokens, "zl", s) for s in FAR]

    def block_start(chip, side, index):
        return (((chip ^ (index & 3)) << 1) + ((index >> 2) ^ side)) * per_row

    chunk = y * X + x
    offset = (chunk & 1) * per_chunk
    source_chip, source_core = (zl >> 1) + 2 * core, zl & 1
    row_start = block_start(zl, core, chunk >> 1) + offset
    key_start = block_start(source_chip, source_core, chunk >> 1) + offset
    starts = [block_start(source_chip, source_core, i) for i in range(8)]
    base = jnp.stack([*starts, row_start, core]).astype(jnp.int32)
    steps = jnp.arange(per_chunk)
    cosine, sine_v = tables((row_start + steps).astype(F32), HD)
    key_cos, key_sin = tables((key_start + steps).astype(F32), HD)
    key_cos = jnp.where(core == 0, key_cos, 1.0)
    key_sin = jnp.where(core == 0, key_sin, 0.0)
    first, second = jnp.where(core == 0, x, y), jnp.where(core == 0, y, x)
    place = jnp.stack([first, second, 1 + 3 * core, 4 - 3 * core]).astype(jnp.int32)

    near = partner(tokens, "core", 1)
    early, early_kv = call(
        early_kernel,
        [(4, per_chunk, width), (4, per_chunk, HD)],
        [tokens, near, w_query, w_keyval],
    )
    *far, early = lax.optimization_barrier((*far, early))
    far += [partner(block, "core", 1) for block in far]
    (kv_parts,) = call(
        keyval_kernel, [(Y * X, per_chunk, HD)], [*far, w_keyval, early_kv]
    )
    parts = call(
        query_kernel,
        [(4, per_chunk, width)] * 4,
        [place, *far, w_query, early],
        [SMEM],
        [pltpu.VMEM((Y * X, per_chunk, width), BF16)],
    )
    kv_parts = lax.all_to_all(kv_parts, PLANE, 0, 0, tiled=True)
    (kv,) = call(sum_kernel, [(per_chunk, HD)], [kv_parts])

    moves = [(e, 2 * (e % 4) + e // 4) for e in range(8)]
    here = lax.ppermute(kv, ROW, moves)
    across = lax.ppermute(
        kv, (*ROW, "zh"), [(2 * e + h, 2 * r + 1 - h) for e, r in moves for h in range(2)]
    )
    (kv_block,) = call(keys_kernel, [(Y * X, per_chunk, HD)], [here, across, key_cos, key_sin])
    got = [across_plane(parts[s], s, False) for s in STEPS[1:]]
    halves = call(
        halve_kernel,
        [jax.ShapeDtypeStruct((per_chunk, width), F32), *[(per_chunk, width)] * 3],
        [place, parts[0], *got],
        [SMEM],
    )
    got = [across_plane(halves[t], t, True) for t in STEPS[1:]]
    kv_own = lax.all_to_all(kv_block, PLANE, 0, 0, tiled=True).reshape(total, HD)
    kv_other = partner(kv_own, "core", 1)
    (own,) = call(join_kernel, [(per_chunk, width)], [halves[0], *got])
    got = partner(own, "zh", 1)

    (attended,) = call(
        functools.partial(attention_kernel, heads),
        [(per_chunk, width)],
        [base, own, got, cosine, sine_v, kv_own, kv_other],
        [SMEM],
        [pltpu.VMEM((heads * per_chunk, HD), BF16), pltpu.VMEM((2, total, HD), BF16)],
    )

    (line,) = call(
        stack_kernel,
        [(4, per_chunk, width)],
        [attended] + [across_plane(attended, s, False) for s in STEPS[1:]],
    )
    gathered = [across_plane(line, t, True) for t in STEPS[1:]]
    early = []
    for block in gathered:
        (done,) = call(line_kernel, [(4, per_chunk, features)], [line, w_output])
        line, done = lax.optimization_barrier((block, done))
        early.append(done)
    kept, sent = call(
        output_kernel,
        [(Y * X // 2, per_chunk, features)] * 2,
        [place, *early, line, w_output],
        [SMEM],
        [
            pltpu.VMEM((4, per_chunk, features), BF16),
            pltpu.VMEM((Y * X, per_chunk, features), BF16),
        ],
    )
    kept, sent = kept.reshape(half, features), sent.reshape(half, features)
    chip = call(chip_kernel, [(per_row, features)] * 4, [kept, partner(sent, "core", 1)])
    blocks = [chip[0]] + [partner(chip[s], "zl", s) for s in FAR]
    (result,) = call(total_kernel, [(per_row, features)], blocks)
    return result


def solution(mesh):
    fine = Mesh(
        mesh.devices.reshape(Z_LO, CORE, Z_HI, Y, X), ("zl", "core", "zh", "y", "x")
    )
    return jax.shard_map(
        shards,
        mesh=fine,
        in_specs=(P(ROW, COL), P(COL, ROW), P(COL, ROW), P(ROW, COL)),
        out_specs=P(ROW, COL),
        check_vma=False,
    )
```
